32 devices in a mesh: groups: 2 (over y), leaf: 4 (over z), sub: 4 (over x, core).
Axes of the slice: x: 2, y: 2, z: 4, core: 2. Of those that a mesh axis runs over, the one named last changes fastest.
Arguments:
- rhs: bfloat16 [32, 65536], P(None, ('groups', 'leaf', 'sub')), parts along dimension 1, may hold values from -6 to 6
- bases: bfloat16 [256, 64, 256], P(('groups', 'leaf', 'sub')), parts along dimension 0, may hold values from -0.375 to 0.375
- near_blocks: bfloat16 [256, 3, 256, 256], P(('groups', 'leaf', 'sub')), parts along dimension 0, may hold values from -0.21875 to 0.21875
- transfer: bfloat16 [12, 2, 64, 64], replicated, may hold values from -0.75 to 0.75
- couple: bfloat16 [12, 4, 64, 64], replicated, may hold values from -0.4375 to 0.4375
- codes: int32 [12, 3, 128], replicated, may hold values from 0 to 4, as said below
Outputs:
- product: bfloat16 [32, 65536], P(None, ('groups', 'leaf', 'sub')), parts along dimension 1
The draws below stay inside these ranges and needn't reach their ends.
There are 2 independent parts, one for each index of `groups`. The reference program is written for one: setup_inputs(seed, part) draws one part's arguments, and reference() takes and returns one part's arrays. A program takes and returns all parts, laid end to end along the dimension named above; an argument that names none is the same for every part. Nothing has to cross between parts.
Inputs may be any that keep to these rules, and one draw needn't show every extreme that they name: For a cluster c of level t (c < 128 / 2**t), codes[t, s, c] in 0 to 3 names the partner c-3, c-2, c+2, c+3 and 4 marks an empty slot; the partners named for one cluster differ; entries of larger c are not read.
All inputs are finite; a program needn't handle non-finite values.
Results may differ from the reference program's by a relative error of at most 0.0044.
Values may be sent and summed in bfloat16 or wider, within the bound.
No kernel may reach another device: no remote copies, remote signals or barrier semaphores. Data moves between devices by JAX's collectives and lax.ppermute only.
A program may use at most 64 MiB of HBM per device.

```python
import jax
import jax.numpy as jnp
from jax import lax

RHS = 32
RANK = 64
LEAF = 256
LEVELS = 12
SLOTS = 3
LEAVES = 128
POINTS = 32768


def draw_codes(key, part):
    key = jax.random.fold_in(key, 11)
    order_key, empty_key = jax.random.split(key)
    scores = jax.random.randint(order_key, (LEVELS, LEAVES, 4), 0, 1 << 20) * 4 + jnp.arange(4, dtype=jnp.int32)
    picks = jnp.argsort(scores, axis=-1, stable=True)[..., :SLOTS].astype(jnp.int32)
    empty = jax.random.randint(empty_key, (LEVELS, LEAVES), 0, 4) == 0
    last_slot = jnp.where(empty, 4, picks[..., SLOTS - 1]).astype(jnp.int32)
    picks = picks.at[..., SLOTS - 1].set(last_slot)
    return jnp.transpose(picks, (0, 2, 1))


def block_scale(key, extent, cuts, low, largest):
    loudness, own = 1.0, jax.random.fold_in(key, 6)
    for position, shards_of in cuts:
        draws = jnp.exp(jax.random.uniform(jax.random.fold_in(own, position), (shards_of,), jnp.float32, low / len(cuts), largest / len(cuts)))
        loudness = loudness * jnp.repeat(draws, extent[position] // shards_of).reshape([-1 if axis == position else 1 for axis in range(len(extent))])
    return loudness


def gaussian(own_key, extent, deviation, reach, cuts=(), held_as=jnp.bfloat16):
    array = jax.random.normal(own_key, extent, jnp.float32) * deviation
    if len(cuts) > 0:
        array = block_scale(own_key, extent, cuts, -0.22, 0.18) * array
    return jnp.clip(array, min=-reach, max=reach).astype(held_as)


def setup_inputs(seed: int = 0, part: int = 0) -> dict:
    keys = jax.random.split(jax.random.key(seed), 7)
    part_keys = jax.random.split(jax.random.fold_in(keys[6], part), 7)
    return {
        "rhs": gaussian(part_keys[0], (RHS, POINTS), 1.0, 6.0, ((1, 16),)),
        "bases": gaussian(part_keys[1], (LEAVES, RANK, LEAF), LEAF ** -0.5, 0.375, ((0, 16),)),
        "near_blocks": gaussian(part_keys[2], (LEAVES, 3, LEAF, LEAF), (3 * LEAF) ** -0.5, 0.21875, ((0, 16),)),
        "transfer": gaussian(keys[3], (LEVELS, 2, RANK, RANK), RANK ** -0.5, 0.75),
        "couple": gaussian(keys[4], (LEVELS, 4, RANK, RANK), (3 * RANK) ** -0.5, 0.4375),
        "codes": draw_codes(jax.random.fold_in(keys[6], 71), part),
    }


ROOT_HALF = 0.7071067811865476
OFFSETS = (-3, -2, 2, 3)


def forward_map(coef, matrix):
    return jnp.einsum("crk,kj->crj", coef, matrix, precision=lax.Precision.HIGHEST)


def backward_map(coef, matrix):
    return jnp.einsum("crj,kj->crk", coef, matrix, precision=lax.Precision.HIGHEST)


def merge_pairs(coef, tables, level):
    return (forward_map(coef[0::2], tables[level, 0]) + forward_map(coef[1::2], tables[level, 1])) * ROOT_HALF


def split_pairs(coef, tables, level):
    left_part = backward_map(coef, tables[level, 0])
    right_part = backward_map(coef, tables[level, 1])
    return jnp.stack([left_part, right_part], axis=1).reshape((2 * coef.shape[0],) + coef.shape[1:])


def apply_couplings(extended, anchor, count, level_codes, table):
    total = jnp.zeros((count,) + extended.shape[1:], jnp.float32)
    for index, offset in enumerate(OFFSETS):
        window = lax.slice_in_dim(extended, anchor + offset, anchor + offset + count, axis=0)
        weight = jnp.sum((level_codes == index).astype(jnp.float32), axis=0)
        total = total + forward_map(window * weight[:, None, None], table[index])
    return total


def couple_padded(level_coef, level_codes, table):
    count = level_coef.shape[0]
    padded = jnp.pad(level_coef, ((3, 3), (0, 0), (0, 0)))
    return apply_couplings(padded, 3, count, level_codes, table)


def top_tree(every, codes, tables, links, base_level, bits):
    upward = [every]
    for bit in range(bits):
        upward.append(merge_pairs(upward[-1], tables, base_level + bit))
    level = base_level + bits
    state = couple_padded(upward[bits], codes[level, :, :upward[bits].shape[0]], links[level])
    for bit in reversed(range(bits)):
        level = base_level + bit
        count = upward[bit].shape[0]
        state = couple_padded(upward[bit], codes[level, :, :count], links[level]) + split_pairs(state, tables, level)
    return state


def reference(rhs, bases, near_blocks, transfer, couple, codes):
    bits = LEAVES.bit_length() - 1
    leaf_rhs = rhs.reshape(RHS, LEAVES, LEAF).astype(jnp.float32)
    bases_wide = bases.astype(jnp.float32)
    coef = jnp.einsum("rlm,lkm->lrk", leaf_rhs, bases_wide, precision=lax.Precision.HIGHEST)
    state = top_tree(coef, codes, transfer.astype(jnp.float32), couple.astype(jnp.float32), 0, bits)
    leaf_coef = state.astype(jnp.bfloat16)
    total = jnp.einsum("lrk,lkm->rlm", leaf_coef.astype(jnp.float32), bases_wide, precision=lax.Precision.HIGHEST)
    padded = jnp.pad(leaf_rhs, ((0, 0), (1, 1), (0, 0)))
    for shift_index in range(3):
        total = total + jnp.einsum("rlm,lnm->rln", padded[:, shift_index:shift_index + LEAVES],
                                   near_blocks[:, shift_index].astype(jnp.float32),
                                   precision=lax.Precision.HIGHEST)
    return total.reshape(RHS, POINTS).astype(jnp.bfloat16)
```

```python
import functools

import jax
import jax.numpy as jnp
from jax import lax
from jax.experimental import pallas as pl
from jax.experimental.pallas import tpu as pltpu
from jax.sharding import PartitionSpec as P

ROOT_HALF = 0.7071067811865476
OFFSETS = (-3, -2, 2, 3)
AXES = ("leaf", "sub")
BF = jnp.bfloat16
F32 = jnp.float32
VMEM = pl.BlockSpec(memory_space=pltpu.VMEM)
SMEM = pl.BlockSpec(memory_space=pltpu.SMEM)


def mm(a, b):
    return lax.dot_general(a, b, (((1,), (0,)), ((), ())), preferred_element_type=F32)


def mm_t(a, b):
    return lax.dot_general(a, b, (((1,), (1,)), ((), ())), preferred_element_type=F32)


def split(a):
    high = a.astype(BF)
    low = (a - high.astype(F32)).astype(BF)
    return jnp.concatenate([high, low], axis=0)


def mm2(a, b, product=mm):
    out = product(split(a), b)
    return out[: a.shape[0]] + out[a.shape[0] :]


def side(*parts):
    return jnp.concatenate(parts, axis=1)


def stack(*parts):
    return jnp.concatenate(parts, axis=0)


def stages_of(devices):
    bits = devices.bit_length() - 1
    return [(b, 2 if b + 1 < bits else 1) for b in range(0, bits, 2)]


def exchanged(x, apart):
    devices = lax.axis_size(AXES)
    return lax.ppermute(x, AXES, [(i, i ^ apart) for i in range(devices)])


def up_kernel(pos, x, bases, transfer, pay_a, pay_c, own0, own1, own2):
    leaves, rank, size = bases.shape
    rows = x.shape[0]
    up = [mm_t(x[:, i * size : (i + 1) * size], bases[i]) for i in range(leaves)]
    pairs = [side(up[i], up[i + 1]) for i in range(0, leaves, 2)]
    u0 = stack(*pairs)
    own0[...] = u0.astype(BF)
    up1 = mm2(u0, transfer[0].reshape(2 * rank, rank)) * ROOT_HALF
    up1 = [up1[i * rows : (i + 1) * rows] for i in range(leaves // 2)]
    pairs1 = [side(up1[i], up1[i + 1]) for i in range(0, leaves // 2, 2)]
    u1 = stack(*pairs1)
    own1[...] = u1.astype(BF)
    up2 = mm2(u1, transfer[1].reshape(2 * rank, rank)) * ROOT_HALF
    u2 = side(up2[:rows], up2[rows:]).astype(BF)
    own2[...] = u2
    half = size // 2
    end = leaves * size
    right = stack(
        x[:, end - size : end - half],
        x[:, end - half : end],
        pairs[-1].astype(BF),
        pairs1[-1].astype(BF),
        side(up[-3], up1[-3]).astype(BF),
    )
    left = stack(
        x[:, :half],
        x[:, half:size],
        pairs[0].astype(BF),
        pairs1[0].astype(BF),
        side(up[2], up1[2]).astype(BF),
    )
    even = pos[0] % 2 == 0
    edge = right.shape[0]
    pay_a[:edge] = jnp.where(even, right, left)
    pay_c[:edge] = jnp.where(even, left, right)
    pay_a[edge:] = u2
    pay_c[edge:] = u2


def near_kernel(devices, pos, codes, x, blocks, near, ends, masks):
    leaf = pl.program_id(0)
    leaves = pl.num_programs(0)
    size = blocks.shape[-1]
    at = lambda i: x[:, pl.ds(pl.multiple_of(i * size, size), size)]
    before = jnp.maximum(leaf - 1, 0)
    after = jnp.minimum(leaf + 1, leaves - 1)
    zero = jnp.zeros((x.shape[0], size), BF)
    total = mm_t(at(leaf), blocks[0, 1])
    total += mm_t(jnp.where(leaf > 0, at(before), zero), blocks[0, 0])
    total += mm_t(jnp.where(leaf < leaves - 1, at(after), zero), blocks[0, 2])
    near[:, pl.ds(pl.multiple_of(leaf * size, size), size)] = total

    @pl.when(leaf == 0)
    def _():
        ends[0] = blocks[0, 0]
        p = pos[0]
        lane = lax.broadcasted_iota(jnp.int32, (1, masks.shape[1]), 1) // (masks.shape[1] // 4)
        offset = jnp.where(lane < 2, lane - 3, lane)
        row = 0
        for level, count in mask_rows(devices, ends_leaves(near, size)):
            total_clusters = devices * count if count > 0 else devices >> -count
            for c in range(max(count, 1)):
                index = p * count + c if count > 0 else p >> -count
                hit = jnp.zeros(lane.shape, jnp.bool_)
                for slot in range(codes.shape[1]):
                    hit = hit | (lane == codes[level, slot, index])
                partner = index + offset
                hit = hit & (partner >= 0) & (partner < total_clusters)
                masks[row : row + 1] = jnp.where(hit, 1.0, 0.0).astype(F32)
                row += 1

    @pl.when(leaf == leaves - 1)
    def _():
        ends[1] = blocks[0, 2]


def ends_leaves(near, size):
    return near.shape[1] // size


def mask_rows(devices, leaves):
    rows = []
    level = 0
    while leaves > 1:
        rows.append((level, leaves))
        leaves //= 2
        level += 1
    k = 0
    while devices >> k >= 4:
        rows.append((level, 1 if k == 0 else -k))
        level += 1
        k += 1
    return rows


def down_kernel(devices, stages, *refs):
    refs = list(refs)
    pos, own0, own1, own2 = refs[:4]
    refs = refs[4:]
    received = []
    for _, radix in stages:
        count = 3 if radix == 2 else 1
        received.append(refs[:count])
        refs = refs[count:]
    masks, couple, transfer, bases, near, ends, out, gathered, *ups = refs
    leaves, rank, size = bases.shape
    rows = own2.shape[0]
    edge = received[0][0].shape[0] - rows
    p = pos[0]
    table = lambda level: transfer[level].reshape(2 * rank, rank)
    links = lambda level: couple[level].reshape(4 * rank, rank)

    gathered[0] = own2[...]
    filled = 1
    for got in received:
        for j, ref in enumerate(got):
            skip = edge if j != 1 else 0
            piece = ref[skip:].reshape(filled, rows, 2 * rank)
            gathered[(j + 1) * filled : (j + 2) * filled] = piece
        filled *= len(got) + 1

    even = p % 2 == 0
    first = received[0][0][:edge]
    other = jnp.zeros_like(first)
    open_ = jnp.bool_(True)
    for number, ((b, radix), got) in enumerate(zip(stages, received)):
        digit = (p >> b) & (2**radix - 1)
        digit = jnp.where(even, digit, 2**radix - 1 - digit)
        if number > 0:
            other = jnp.where(open_ & (digit % 2 == 1), got[0][:edge], other)
        if radix == 2:
            other = jnp.where(open_ & (digit == 2), got[2][:edge], other)
        open_ = open_ & (digit == 0)
    left = jnp.where(even, other, first)
    right = jnp.where(even, first, other)

    flat = gathered[...].reshape(devices * rows, 2 * rank)
    level = 3
    up = mm(flat, table(2)) * ROOT_HALF
    count = devices
    ups[0][...] = up.reshape(count, rows, rank)
    for k in range(1, len(ups)):
        bit = (p >> (k - 1)) & 1
        pairs = up.reshape(count // 2, 2, rows, rank)
        count //= 2
        even_part = pairs[:, 0].reshape(count * rows, rank)
        odd_part = pairs[:, 1].reshape(count * rows, rank)
        turned = stack(transfer[level, bit], transfer[level, 1 - bit])
        up = mm2(side(even_part, odd_part), turned) * ROOT_HALF
        ups[k][...] = up.reshape(count, rows, rank)
        level += 1

    row = leaves + leaves // 2 + leaves // 4
    fars = []
    for k in range(len(ups)):
        a = p >> k
        n = devices >> k
        parts = [ups[k][a ^ jnp.clip(a + o, 0, n - 1)] for o in OFFSETS]
        masked = side(*parts) * masks[row + k : row + k + 1]
        fars.append(mm2(masked, links(3 + k)))

    state = fars[-1]
    for k in reversed(range(len(ups) - 1)):
        state = fars[k] + mm2(state, transfer[3 + k, (p >> k) & 1], mm_t)

    at = lambda o: gathered[p ^ jnp.clip(p + o, 0, devices - 1)]
    b2, b1, a1, a2 = at(-2), at(-1), at(1), at(2)
    m = lambda c: masks[c : c + 1].astype(BF)
    row = leaves + leaves // 2
    lhs = stack(
        side(b2[:, rank:], b1[:, :rank], a1) * m(row),
        side(b1, a1[:, rank:], a2[:, :rank]) * m(row + 1),
    )
    far = mm(lhs, links(2))
    state = mm2(state, table(2), mm_t)
    state = far + stack(state[:, :rank], state[:, rank:])

    lo = slice(0, rank)
    hi = slice(rank, 2 * rank)
    s = slice(edge - 2 * rows, edge - rows)
    t = slice(edge - rows, edge)
    ext = [left[t, hi], left[s, lo], left[s, hi]]
    for j in range(leaves // 4):
        ext += [own1[j * rows : (j + 1) * rows, lo], own1[j * rows : (j + 1) * rows, hi]]
    ext += [right[s, lo], right[s, hi], right[t, hi]]
    row = leaves
    lhs = [
        side(*[ext[c + 3 + o] for o in OFFSETS]) * m(row + c) for c in range(leaves // 2)
    ]
    far = mm(stack(*lhs), links(1))
    state = mm2(state, table(1), mm_t)
    state = far + stack(*[state[c // 2 * rows : (c // 2 + 1) * rows, (lo, hi)[c % 2]] for c in range(leaves // 2)])

    s = slice(edge - 3 * rows, edge - 2 * rows)
    ext = [left[t, lo], left[s, lo], left[s, hi]]
    for j in range(leaves // 2):
        ext += [own0[j * rows : (j + 1) * rows, lo], own0[j * rows : (j + 1) * rows, hi]]
    ext += [right[s, lo], right[s, hi], right[t, lo]]
    lhs = [side(*[ext[c + 3 + o] for o in OFFSETS]) * m(c) for c in range(leaves)]
    far = mm(stack(*lhs), links(0))
    state = mm2(state, table(0), mm_t)
    x_left = side(left[:rows], left[rows : 2 * rows])
    x_right = side(right[:rows], right[rows : 2 * rows])
    for c in range(leaves):
        coef = state[c // 2 * rows : (c // 2 + 1) * rows, (lo, hi)[c % 2]] + far[c * rows : (c + 1) * rows]
        cols = slice(c * size, (c + 1) * size)
        total = mm(coef.astype(BF), bases[c]) + near[:, cols]
        if c == 0:
            total += mm_t(x_left, ends[0])
        if c == leaves - 1:
            total += mm_t(x_right, ends[1])
        out[:, cols] = total.astype(BF)


def shards(rhs, bases, near_blocks, transfer, couple, codes):
    rows = rhs.shape[0]
    leaves, rank, size = bases.shape
    devices = lax.axis_size(AXES)
    stages = stages_of(devices)
    pos = lax.axis_index(AXES).astype(jnp.int32).reshape(1)
    edge = 5 * rows
    pay = jax.ShapeDtypeStruct((edge + rows, 2 * rank), BF)
    pay_a, pay_c, own0, own1, own2 = pl.pallas_call(
        up_kernel,
        out_shape=[
            pay,
            pay,
            jax.ShapeDtypeStruct((leaves // 2 * rows, 2 * rank), BF),
            jax.ShapeDtypeStruct((leaves // 4 * rows, 2 * rank), BF),
            jax.ShapeDtypeStruct((rows, 2 * rank), BF),
        ],
        grid=(1,),
        in_specs=[
            SMEM,
            pl.BlockSpec(rhs.shape, lambda i: (0, 0)),
            pl.BlockSpec(bases.shape, lambda i: (0, 0, 0)),
            pl.BlockSpec((2, 2, rank, rank), lambda i: (0, 0, 0, 0)),
        ],
        out_specs=[VMEM] * 5,
        name="up_sweep",
    )(pos, rhs, bases, transfer)

    row_count = sum(max(count, 1) for _, count in mask_rows(devices, leaves))
    near, ends, masks = pl.pallas_call(
        functools.partial(near_kernel, devices),
        out_shape=[
            jax.ShapeDtypeStruct((rows, leaves * size), F32),
            jax.ShapeDtypeStruct((2, size, size), BF),
            jax.ShapeDtypeStruct((-(-row_count // 8) * 8, 4 * rank), F32),
        ],
        grid=(leaves,),
        in_specs=[
            SMEM,
            SMEM,
            VMEM,
            pl.BlockSpec((1, 3, size, size), lambda i: (i, 0, 0, 0)),
        ],
        out_specs=[VMEM] * 3,
        name="near_field",
        cost_estimate=pl.CostEstimate(flops=3 * leaves * rows * size * size * 2, bytes_accessed=3 * leaves * size * size * 2, transcendentals=0),
    )(pos, codes, rhs, near_blocks)

    received = []
    gathered = own2
    relay = None
    for b, radix in stages:
        if relay is not None:
            pay_a = pay_c = stack(relay, gathered)
        if radix == 1:
            got = [exchanged(pay_a, 1 << b)]
        else:
            got = [exchanged(pay_a, 1 << b), exchanged(gathered, 2 << b), exchanged(pay_c, 3 << b)]
        received.append(got)
        relay = got[-1][:edge]
        gathered = stack(gathered, *[g[edge:] if j != 1 else g for j, g in enumerate(got)])

    levels = [k for k in range(devices.bit_length()) if devices >> k >= 4]
    flat = [g for got in received for g in got]
    operands = [own0, own1, own2, *flat, masks, couple, transfer, bases, near, ends]
    return pl.pallas_call(
        functools.partial(down_kernel, devices, stages),
        out_shape=jax.ShapeDtypeStruct((rows, leaves * size), BF),
        in_specs=[SMEM] + [VMEM] * len(operands),
        out_specs=VMEM,
        scratch_shapes=[pltpu.VMEM((devices, rows, 2 * rank), BF)]
        + [pltpu.VMEM((devices >> k, rows, rank), F32) for k in levels],
        name="down_sweep",
    )(pos, *operands)


def solution(mesh):
    return jax.shard_map(
        shards,
        mesh=mesh,
        in_specs=(
            P(None, ("groups", "leaf", "sub")),
            P(("groups", "leaf", "sub"), None, None),
            P(("groups", "leaf", "sub"), None, None, None),
            P(),
            P(),
            P(),
        ),
        out_specs=P(None, ("groups", "leaf", "sub")),
        check_vma=False,
    )
```

```python
import functools

import jax
import jax.numpy as jnp
from jax import lax
from jax.experimental import pallas as pl
from jax.experimental.pallas import tpu as pltpu
from jax.sharding import PartitionSpec as P

ROOT_HALF = 0.7071067811865476
OFFSETS = (-3, -2, 2, 3)
AXES = ("leaf", "sub")
BF = jnp.bfloat16
F32 = jnp.float32


def mm(a, b):
    return lax.dot_general(a, b, (((1,), (0,)), ((), ())), preferred_element_type=F32)


def mm_t(a, b):
    return lax.dot_general(a, b, (((1,), (1,)), ((), ())), preferred_element_type=F32)


def split(a):
    high = a.astype(BF)
    low = (a - high.astype(F32)).astype(BF)
    return jnp.concatenate([high, low], axis=0)


def mm2(a, b, product=mm):
    out = product(split(a), b)
    return out[: a.shape[0]] + out[a.shape[0] :]


def side(*parts):
    return jnp.concatenate(parts, axis=1)


def stack(*parts):
    return jnp.concatenate(parts, axis=0)


def stages_of(devices):
    bits = [1 << b for b in range(1, devices.bit_length() - 1)]
    rounds = []
    while len(bits) > 1:
        low, high, *bits = bits
        rounds.append((low, high, low | high))
    return rounds + [(b,) for b in bits] + [(1,)]


def slots_of(stages):
    held = [[0]]
    for masks in stages:
        held.append(held[-1] + [slot ^ m for m in masks for slot in held[-1]])
    return held


def exchanged(x, apart):
    devices = lax.axis_size(AXES)
    return lax.ppermute(x, AXES, [(i, i ^ apart) for i in range(devices)])


def load_kernel(count, *refs):
    copies = [
        pltpu.make_async_copy(refs[i], refs[count + i], refs[-1].at[i]) for i in range(count)
    ]
    for copy in copies:
        copy.start()
    for copy in copies:
        copy.wait()


def up_kernel(x, bases, transfer, facing, away, own0, own1, own2):
    leaves, rank, size = bases.shape
    rows = x.shape[0]
    up = [mm_t(x[:, i * size : (i + 1) * size], bases[i]) for i in range(leaves)]
    pairs = [side(up[i], up[i + 1]) for i in range(0, leaves, 2)]
    u0 = stack(*pairs)
    own0[...] = u0.astype(BF)
    up1 = mm2(u0, transfer[0].reshape(2 * rank, rank)) * ROOT_HALF
    up1 = [up1[i * rows : (i + 1) * rows] for i in range(leaves // 2)]
    pairs1 = [side(up1[i], up1[i + 1]) for i in range(0, leaves // 2, 2)]
    u1 = stack(*pairs1)
    own1[...] = u1.astype(BF)
    up2 = mm2(u1, transfer[1].reshape(2 * rank, rank)) * ROOT_HALF
    own2[...] = side(up2[:rows], up2[rows:]).astype(BF)
    half = size // 2
    end = leaves * size
    right = stack(
        x[:, end - size : end - half],
        x[:, end - half : end],
        pairs[-1].astype(BF),
        pairs1[-1].astype(BF),
        side(up[-3], up1[-3]).astype(BF),
    )
    left = stack(
        x[:, :half],
        x[:, half:size],
        pairs[0].astype(BF),
        pairs1[0].astype(BF),
        side(up[2], up1[2]).astype(BF),
    )
    even = lax.axis_index(AXES) % 2 == 0
    facing[...] = jnp.where(even, right, left)
    away[...] = jnp.where(even, left, right)


def pack_kernel(after, *refs):
    *parts, out = refs
    at = 0
    for part in parts:
        out[at : at + part.shape[0]] = part[...]
        at += part.shape[0]


def near_kernel(codes, x, blocks, near, ends, masks):
    leaves, _, size, _ = blocks.shape
    at = lambda i: x[:, i * size : (i + 1) * size]
    for i in range(leaves):
        total = mm_t(at(i), blocks[i, 1])
        if i > 0:
            total += mm_t(at(i - 1), blocks[i, 0])
        if i < leaves - 1:
            total += mm_t(at(i + 1), blocks[i, 2])
        near[:, i * size : (i + 1) * size] = total
    ends[0] = blocks[0, 0]
    ends[1] = blocks[leaves - 1, 2]

    p = lax.axis_index(AXES)
    wide = codes.shape[2]
    quarter = masks.shape[1] // 4
    across = lax.broadcasted_iota(jnp.int32, (8, masks.shape[1]), 1) // quarter
    offset = jnp.where(across < 2, across - 3, across)
    cluster = lax.broadcasted_iota(jnp.int32, (8, masks.shape[1]), 0)
    diagonal = lax.broadcasted_iota(jnp.int32, (8, wide), 0) == lax.broadcasted_iota(jnp.int32, (8, wide), 1)
    for level in range(masks.shape[0] // 8):
        count = leaves >> level
        index = p * count if count > 0 else p >> level - (leaves.bit_length() - 1)
        clusters = wide >> level
        hit = jnp.zeros(across.shape, jnp.bool_)
        for slot in range(codes.shape[1]):
            row = jnp.broadcast_to(codes[level, slot : slot + 1], (8, wide))
            row = pltpu.roll(row, lax.rem(wide - index, wide), 1)
            code = jnp.sum(jnp.where(diagonal, row, 0).astype(F32), axis=1, keepdims=True)
            hit = hit | (across.astype(F32) == code)
        partner = index + cluster + offset
        hit = hit & (partner >= 0) & (partner < clusters)
        masks[8 * level : 8 * level + 8] = jnp.where(hit, 1.0, 0.0)


def climb(up, count, transfer, level, bit, rows):
    rank = up.shape[1]
    pairs = up.reshape(count // 2, 2, rows, rank)
    halves = [pairs[:, i].reshape(count // 2 * rows, rank) for i in range(2)]
    turned = stack(transfer[level, bit], transfer[level, 1 - bit])
    return mm2(side(*halves), turned) * ROOT_HALF


def down_kernel(devices, stages, *refs):
    refs = list(refs)
    own0, own1, own2, across = refs[:4]
    refs = refs[4:]
    received = []
    for group in stages:
        received.append(refs[: len(group)])
        refs = refs[len(group) :]
    masks, couple, transfer, bases, near, ends, out, gathered, *ups = refs
    leaves, rank, size = bases.shape
    rows = own2.shape[0]
    edge = across.shape[0]
    p = lax.axis_index(AXES)
    table = lambda level: transfer[level].reshape(2 * rank, rank)
    links = lambda level: couple[level].reshape(4 * rank, rank)

    gathered[0] = own2[...]
    for group, got, held in zip(stages, received, slots_of(stages)):
        for m, ref in zip(group, got):
            skip = edge if m == 1 else 0
            for i, slot in enumerate(held):
                at = skip + i * rows
                gathered[slot ^ m] = ref[at : at + rows]

    even = p % 2 == 0
    first = received[-1][0][:edge]
    other = across[...]
    left = jnp.where(even, other, first)
    right = jnp.where(even, first, other)

    count = devices
    up = mm(gathered[...].reshape(devices * rows, 2 * rank), table(2)) * ROOT_HALF
    ups[0][...] = up.reshape(count, rows, rank)
    for k in range(1, len(ups)):
        up = climb(up, count, transfer, 2 + k, (p >> (k - 1)) & 1, rows)
        count //= 2
        ups[k][...] = up.reshape(count, rows, rank)

    fars = []
    for k in range(len(ups)):
        a = p >> k
        n = devices >> k
        parts = [ups[k][a ^ jnp.clip(a + o, 0, n - 1)] for o in OFFSETS]
        masked = side(*parts) * masks[8 * (3 + k) : 8 * (3 + k) + 1]
        fars.append(mm2(masked, links(3 + k)))

    state = fars[-1]
    for k in reversed(range(len(ups) - 1)):
        state = fars[k] + mm2(state, transfer[3 + k, (p >> k) & 1], mm_t)

    at = lambda o: gathered[p ^ jnp.clip(p + o, 0, devices - 1)]
    b2, b1, a1, a2 = at(-2), at(-1), at(1), at(2)
    m = lambda c: masks[c : c + 1].astype(BF)
    row = 16
    lhs = stack(
        side(b2[:, rank:], b1[:, :rank], a1) * m(row),
        side(b1, a1[:, rank:], a2[:, :rank]) * m(row + 1),
    )
    far = mm(lhs, links(2))
    state = mm2(state, table(2), mm_t)
    state = far + stack(state[:, :rank], state[:, rank:])

    lo = slice(0, rank)
    hi = slice(rank, 2 * rank)
    s = slice(edge - 2 * rows, edge - rows)
    t = slice(edge - rows, edge)
    ext = [left[t, hi], left[s, lo], left[s, hi]]
    for j in range(leaves // 4):
        ext += [own1[j * rows : (j + 1) * rows, lo], own1[j * rows : (j + 1) * rows, hi]]
    ext += [right[s, lo], right[s, hi], right[t, hi]]
    row = 8
    lhs = [
        side(*[ext[c + 3 + o] for o in OFFSETS]) * m(row + c) for c in range(leaves // 2)
    ]
    far = mm(stack(*lhs), links(1))
    state = mm2(state, table(1), mm_t)
    state = far + stack(*[state[c // 2 * rows : (c // 2 + 1) * rows, (lo, hi)[c % 2]] for c in range(leaves // 2)])

    s = slice(edge - 3 * rows, edge - 2 * rows)
    ext = [left[t, lo], left[s, lo], left[s, hi]]
    for j in range(leaves // 2):
        ext += [own0[j * rows : (j + 1) * rows, lo], own0[j * rows : (j + 1) * rows, hi]]
    ext += [right[s, lo], right[s, hi], right[t, lo]]
    lhs = [side(*[ext[c + 3 + o] for o in OFFSETS]) * m(c) for c in range(leaves)]
    far = mm(stack(*lhs), links(0))
    state = mm2(state, table(0), mm_t)
    x_left = side(left[:rows], left[rows : 2 * rows])
    x_right = side(right[:rows], right[rows : 2 * rows])
    for c in range(leaves):
        coef = state[c // 2 * rows : (c // 2 + 1) * rows, (lo, hi)[c % 2]] + far[c * rows : (c + 1) * rows]
        cols = slice(c * size, (c + 1) * size)
        total = mm(coef.astype(BF), bases[c]) + near[:, cols]
        if c == 0:
            total += mm_t(x_left, ends[0])
        if c == leaves - 1:
            total += mm_t(x_right, ends[1])
        out[:, cols] = total.astype(BF)


def inside(x):
    return pltpu.with_memory_space_constraint(x, pltpu.VMEM)


def outside(x):
    return pltpu.with_memory_space_constraint(x, pltpu.HBM)


def shards(rhs, bases, near_blocks, transfer, couple, codes):
    rows = rhs.shape[0]
    leaves, rank, size = bases.shape
    devices = lax.axis_size(AXES)
    stages = stages_of(devices)
    edge = 5 * rows
    params = pltpu.CompilerParams(vmem_limit_bytes=16 << 20)
    anywhere = pl.BlockSpec(memory_space=pl.ANY)
    loaded = (rhs, bases, transfer, codes)
    x, bases, transfer, codes = pl.pallas_call(
        functools.partial(load_kernel, len(loaded)),
        out_shape=[pltpu.VMEM(a.shape, a.dtype) for a in loaded],
        in_specs=[anywhere] * len(loaded),
        scratch_shapes=[pltpu.SemaphoreType.DMA((len(loaded),))],
        compiler_params=params,
        name="load",
    )(*map(outside, loaded))

    facing, away, own0, own1, own2 = pl.pallas_call(
        up_kernel,
        out_shape=[
            pltpu.VMEM((edge, 2 * rank), BF),
            pltpu.VMEM((edge, 2 * rank), BF),
            pltpu.VMEM((leaves // 2 * rows, 2 * rank), BF),
            pltpu.VMEM((leaves // 4 * rows, 2 * rank), BF),
            pltpu.VMEM((rows, 2 * rank), BF),
        ],
        compiler_params=params,
        cost_estimate=pl.CostEstimate(flops=1 << 32, bytes_accessed=1 << 20, transcendentals=0),
        name="up_sweep",
    )(*map(inside, (x, bases, transfer)))

    levels = [k for k in range(devices.bit_length()) if devices >> k >= 4]
    near, ends, masks = pl.pallas_call(
        near_kernel,
        out_shape=[
            pltpu.VMEM((rows, leaves * size), F32),
            pltpu.VMEM((2, size, size), BF),
            pltpu.VMEM((8 * (3 + len(levels)), 4 * rank), F32),
        ],
        compiler_params=params,
        name="near_field",
        cost_estimate=pl.CostEstimate(
            flops=3 * leaves * rows * size * size * 2,
            bytes_accessed=3 * leaves * size * size * 2,
            transcendentals=0,
        ),
    )(*map(inside, (codes, x, near_blocks)))

    across = [(i, i + 1) for i in range(1, devices - 1, 2)]
    across = lax.ppermute(away, AXES, across + [(j, i) for i, j in across])
    received = []
    gathered = own2
    for group in stages:
        if group is not stages[-1]:
            got = [exchanged(gathered, m) for m in group]
            if group is not stages[-2]:
                gathered = stack(gathered, *got)
        else:
            parts = (facing, gathered, *(received[-1] if received else ()))
            size_all = sum(part.shape[0] for part in parts)
            pay = pl.pallas_call(
                pack_kernel,
                out_shape=pltpu.VMEM((size_all, 2 * rank), BF),
                compiler_params=params,
                name="pack",
            )(*map(inside, (across, *parts)))
            got = [exchanged(pay, 1)]
        received.append(got)

    flat = [g for got in received for g in got]
    operands = [own0, own1, own2, across, *flat, masks, couple, transfer, bases, near, ends]
    return pl.pallas_call(
        functools.partial(down_kernel, devices, stages),
        out_shape=jax.ShapeDtypeStruct((rows, leaves * size), BF),
        scratch_shapes=[pltpu.VMEM((devices, rows, 2 * rank), BF)]
        + [pltpu.VMEM((devices >> k, rows, rank), F32) for k in levels],
        compiler_params=params,
        name="down_sweep",
    )(*map(inside, operands))


def solution(mesh):
    return jax.shard_map(
        shards,
        mesh=mesh,
        in_specs=(
            P(None, ("groups", "leaf", "sub")),
            P(("groups", "leaf", "sub"), None, None),
            P(("groups", "leaf", "sub"), None, None, None),
            P(),
            P(),
            P(),
        ),
        out_specs=P(None, ("groups", "leaf", "sub")),
        check_vma=False,
    )
```

```python
import functools

import jax
import jax.numpy as jnp
from jax import lax
from jax.experimental import pallas as pl
from jax.experimental.pallas import tpu as pltpu
from jax.sharding import PartitionSpec as P

ROOT_HALF = 0.7071067811865476
OFFSETS = (-3, -2, 2, 3)
AXES = ("leaf", "sub")
BF = jnp.bfloat16
F32 = jnp.float32
LANES = 64


def mm(a, b):
    return lax.dot_general(a, b, (((1,), (0,)), ((), ())), preferred_element_type=F32)


def mm_t(a, b):
    return lax.dot_general(a, b, (((1,), (1,)), ((), ())), preferred_element_type=F32)


def split(a):
    high = a.astype(BF)
    low = (a - high.astype(F32)).astype(BF)
    return jnp.concatenate([high, low], axis=0)


def mm2(a, b, product=mm):
    out = product(split(a), b)
    return out[: a.shape[0]] + out[a.shape[0] :]


def halves(a, axis):
    high = a.astype(BF)
    return jnp.concatenate([high, (a - high.astype(F32)).astype(BF)], axis=axis)


def side(*parts):
    return jnp.concatenate(parts, axis=1)


def stack(*parts):
    return jnp.concatenate(parts, axis=0)


def stages_of(devices):
    bits = [1 << b for b in range(1, devices.bit_length() - 1)]
    rounds = [(bits.pop() | 1,)] if len(bits) % 2 else []
    while bits:
        high, low = bits.pop(), bits.pop()
        rounds.append((low | 1, high | 1, low | high))
    return rounds + [(1,)]


def slots_of(stages):
    held = [[0]]
    for masks in stages:
        held.append(held[-1] + [slot ^ m for m in masks for slot in held[-1]])
    return held


def exchanged(x, apart):
    devices = lax.axis_size(AXES)
    return lax.ppermute(x, AXES, [(i, i ^ apart) for i in range(devices)])


def across_pairs(x):
    groups, devices = lax.axis_size("groups"), lax.axis_size(AXES)
    pairs = []
    for g in range(groups):
        for i in range(devices):
            j = i + 1 if i % 2 else i - 1
            to = (g, j) if 0 <= j < devices else ((g + 1) % groups, i)
            pairs.append((g * devices + i, to[0] * devices + to[1]))
    return lax.ppermute(x, ("groups", *AXES), pairs)


def load_kernel(count, *refs):
    copies = [
        pltpu.make_async_copy(refs[i], refs[count + i], refs[-1].at[i]) for i in range(count)
    ]
    for copy in copies:
        copy.start()
    for copy in copies:
        copy.wait()


def up_kernel(x, bases, transfer, facing, away, own0, own1, own2):
    leaves, rank, size = bases.shape
    rows = x.shape[0]
    up = [mm_t(x[:, i * size : (i + 1) * size], bases[i]) for i in range(leaves)]
    pairs = [side(up[i], up[i + 1]) for i in range(0, leaves, 2)]
    u0 = stack(*pairs)
    own0[...] = u0.astype(BF)
    up1 = mm2(u0, transfer[0].reshape(2 * rank, rank)) * ROOT_HALF
    up1 = [up1[i * rows : (i + 1) * rows] for i in range(leaves // 2)]
    pairs1 = [side(up1[i], up1[i + 1]) for i in range(0, leaves // 2, 2)]
    u1 = stack(*pairs1)
    own1[...] = u1.astype(BF)
    up2 = mm2(u1, transfer[1].reshape(2 * rank, rank)) * ROOT_HALF
    u2 = side(up2[:rows], up2[rows:]).astype(BF)
    own2[...] = u2
    half = size // 2
    end = leaves * size
    right = stack(
        x[:, end - size : end - half],
        x[:, end - half : end],
        pairs[-1].astype(BF),
        pairs1[-1].astype(BF),
        side(up[-3], up1[-3]).astype(BF),
        u2,
    )
    left = stack(
        x[:, :half],
        x[:, half:size],
        pairs[0].astype(BF),
        pairs1[0].astype(BF),
        side(up[2], up1[2]).astype(BF),
        u2,
    )
    even = lax.axis_index(AXES) % 2 == 0
    facing[...] = jnp.where(even, right, left)
    away[...] = jnp.where(even, left, right)


def pack_kernel(after, *refs):
    *parts, out = refs
    at = 0
    for part in parts:
        out[at : at + part.shape[0]] = part[...]
        at += part.shape[0]


def sides_of(facing, away):
    p = lax.axis_index(AXES)
    even = p % 2 == 0
    away = jnp.where((p > 0) & (p < lax.axis_size(AXES) - 1), away, jnp.zeros_like(away))
    return jnp.where(even, away, facing), jnp.where(even, facing, away)


def near_kernel(facing, away, x, blocks, near):
    leaves, _, size, _ = blocks.shape
    rows = x.shape[0]
    left, right = sides_of(facing[: 2 * rows], away[: 2 * rows])
    before = side(left[:rows], left[rows:])
    after = side(right[:rows], right[rows:])
    at = lambda i: before if i < 0 else after if i == leaves else x[:, i * size : (i + 1) * size]
    for i in range(leaves):
        total = mm_t(at(i), blocks[i, 1])
        total += mm_t(at(i - 1), blocks[i, 0])
        total += mm_t(at(i + 1), blocks[i, 2])
        near[:, i * size : (i + 1) * size] = total


def mask_of(codes, level, leaves):
    p = lax.axis_index(AXES)
    wide = codes.shape[2]
    lanes = lax.broadcasted_iota(jnp.int32, (8, 4 * LANES), 1) // LANES
    offset = jnp.where(lanes < 2, lanes - 3, lanes)
    cluster = lax.broadcasted_iota(jnp.int32, (8, 4 * LANES), 0)
    diagonal = lax.broadcasted_iota(jnp.int32, (8, wide), 0) == lax.broadcasted_iota(jnp.int32, (8, wide), 1)
    count = leaves >> level
    index = p * count if count > 0 else p >> level - (leaves.bit_length() - 1)
    hit = jnp.zeros(lanes.shape, jnp.bool_)
    for slot in range(codes.shape[1]):
        row = jnp.broadcast_to(codes[level, slot : slot + 1], (8, wide))
        row = pltpu.roll(row, lax.rem(wide - index, wide), 1)
        code = jnp.sum(jnp.where(diagonal, row, 0).astype(F32), axis=1, keepdims=True)
        hit = hit | (lanes.astype(F32) == code)
    partner = index + cluster + offset
    hit = hit & (partner >= 0) & (partner < wide >> level)
    return jnp.where(hit, 1.0, 0.0)


def plan_kernel(
    levels, facing, away, own0, own1, own2, codes, transfer, couple, state, spread, links_out, masks, *lifts
):
    rows = own2.shape[0]
    rank = transfer.shape[-1]
    leaves = own0.shape[0] // rows * 2
    p = lax.axis_index(AXES)
    table = lambda level: transfer[level].reshape(2 * rank, rank)
    links = lambda level: couple[level].reshape(4 * rank, rank)
    lo = slice(0, rank)
    hi = slice(rank, 2 * rank)
    left, right = sides_of(facing[...], away[...])
    block = lambda a, i: a[i * rows : (i + 1) * rows]

    mask = [mask_of(codes, level, leaves) for level in range(3 + levels)]
    masks[:8] = mask[2]
    for k in range(levels):
        masks[8 * (k + 1) : 8 * (k + 2)] = mask[3 + k]

    def coupled(level, ext, count):
        weights = mask[level].astype(BF)
        lhs = [side(*[ext[c + 3 + o] for o in OFFSETS]) * weights[c : c + 1] for c in range(count)]
        return mm(stack(*lhs), links(level))

    zero = jnp.zeros((rows, rank), BF)
    ext = [zero, block(left, 5)[:, lo], block(left, 5)[:, hi], zero, zero]
    ext += [block(right, 5)[:, lo], block(right, 5)[:, hi], zero]
    far2 = coupled(2, ext, 2)
    ext = [block(left, 4)[:, hi], block(left, 3)[:, lo], block(left, 3)[:, hi]]
    ext += [block(own1, c // 2)[:, (lo, hi)[c % 2]] for c in range(leaves // 2)]
    ext += [block(right, 3)[:, lo], block(right, 3)[:, hi], block(right, 4)[:, hi]]
    far1 = coupled(1, ext, leaves // 2)
    ext = [block(left, 4)[:, lo], block(left, 2)[:, lo], block(left, 2)[:, hi]]
    ext += [block(own0, c // 2)[:, (lo, hi)[c % 2]] for c in range(leaves)]
    ext += [block(right, 2)[:, lo], block(right, 2)[:, hi], block(right, 4)[:, lo]]
    far0 = coupled(0, ext, leaves)

    def lowered(value, level, size):
        out = mm2(value, table(level), mm_t)
        return stack(*[out[c // 2 * size : (c // 2 + 1) * size, (lo, hi)[c % 2]] for c in range(2 * (out.shape[0] // size))])

    down = far0 + lowered(far1 + lowered(far2, 1, rows), 0, rows)
    state[...] = side(*[block(down, c) for c in range(leaves)])

    first = couple[2, 0].astype(F32)
    second = couple[2, 3].astype(F32)
    eye = lowered(transfer[2, 0].astype(F32).T, 1, rank)
    one = lowered(transfer[2, 1].astype(F32).T, 1, rank)
    both = lowered(stack(eye, one), 0, rank)
    both = side(*[both[c * rank : (c + 1) * rank] for c in range(leaves)])
    high = both.astype(BF)
    spread[:rank] = high
    spread[rank : 2 * rank] = high
    spread[2 * rank : 3 * rank] = (both - high.astype(F32)).astype(BF)
    half = leaves // 2
    for i, start in enumerate((first, second)):
        out = lowered(lowered(start, 1, rank), 0, rank)
        out = side(*[out[c * rank : (c + 1) * rank] for c in range(half)]).astype(BF)
        none = jnp.zeros_like(out)
        spread[(3 + i) * rank : (4 + i) * rank] = side(out, none) if i == 0 else side(none, out)

    for k in range(levels):
        value = links(3 + k).astype(F32)
        for i in reversed(range(k)):
            value = mm2(value, transfer[3 + i, (p >> i) & 1], mm_t)
        links_out[4 * rank * k : 4 * rank * (k + 1)] = halves(value, 1)

    parts = [table(2).astype(F32) * ROOT_HALF]
    for k, lift in enumerate(lifts):
        b = (p >> k) & 1
        parts = [mm2(a, transfer[3 + k, bit]) * ROOT_HALF for bit in (b, 1 - b) for a in parts]
        lift[...] = halves(stack(*parts), 1)


def climb(up, count, transfer, level, bit, rows):
    rank = up.shape[1]
    pairs = up.reshape(count // 2, 2, rows, rank)
    children = [pairs[:, i].reshape(count // 2 * rows, rank) for i in range(2)]
    turned = stack(transfer[level, bit], transfer[level, 1 - bit])
    return mm2(side(*children), turned) * ROOT_HALF


def down_kernel(devices, stages, levels, *refs):
    refs = list(refs)
    own2 = refs.pop(0)
    received = []
    for group in stages:
        received.append(refs[: len(group)])
        refs = refs[len(group) :]
    lifts = [refs.pop(0) for _ in range(min(levels - 1, 2))]
    state, spread, links, masks, transfer, bases, near, out, gathered, *ups = refs
    leaves, rank, size = bases.shape
    rows = own2.shape[0]
    p = lax.axis_index(AXES)

    gathered[0] = own2[...]
    for group, got, held in zip(stages, received, slots_of(stages)):
        for m, ref in zip(group, got):
            for i, slot in enumerate(held):
                gathered[slot ^ m] = ref[i * rows : (i + 1) * rows]

    every = gathered[...]
    for k in range(levels):
        count = devices >> k
        if k == 0:
            up = mm(every.reshape(devices * rows, 2 * rank), transfer[2].reshape(2 * rank, rank)) * ROOT_HALF
        elif k <= len(lifts):
            sets = every.reshape(count, 1 << k, rows, 2 * rank)
            sets = side(*[sets[:, i].reshape(count * rows, 2 * rank) for i in range(1 << k)])
            up = mm(sets, lifts[k - 1][...])
            up = up[:, :rank] + up[:, rank:]
        else:
            up = climb(up, 2 * count, transfer, 2 + k, (p >> (k - 1)) & 1, rows)
        ups[k][...] = up.reshape(count, rows, rank)

    lhs = []
    for k in range(levels):
        a = p >> k
        n = devices >> k
        parts = [ups[k][a ^ jnp.clip(a + o, 0, n - 1)] for o in OFFSETS]
        lhs.append(side(*parts) * masks[8 * (k + 1) : 8 * (k + 1) + 1])
    top = mm(halves(side(*lhs), 0), links[...])
    top = top[:rows, :rank] + top[:rows, rank:] + top[rows:, :rank] + top[rows:, rank:]

    at = lambda o: gathered[p ^ jnp.clip(p + o, 0, devices - 1)]
    weights = masks[:8].astype(BF)
    before = at(-2)[:, rank:] * weights[0:1, :rank]
    after = at(2)[:, :rank] * weights[1:2, 3 * rank :]
    lhs = side(halves(top, 1), top.astype(BF), before, after)
    coef = (mm(lhs, spread[...]) + state[...]).astype(BF)
    for c in range(leaves):
        cols = slice(c * size, (c + 1) * size)
        out[:, cols] = (mm(coef[:, c * rank : (c + 1) * rank], bases[c]) + near[:, cols]).astype(BF)


def inside(x):
    return pltpu.with_memory_space_constraint(x, pltpu.VMEM)


def outside(x):
    return pltpu.with_memory_space_constraint(x, pltpu.HBM)


def shards(rhs, bases, near_blocks, transfer, couple, codes):
    rows = rhs.shape[0]
    leaves, rank, size = bases.shape
    devices = lax.axis_size(AXES)
    stages = stages_of(devices)
    levels = devices.bit_length() - 2
    params = pltpu.CompilerParams(vmem_limit_bytes=16 << 20)

    def call(kernel, shapes, operands, name, flops=0, place=inside, **more):
        single = not isinstance(shapes, list)
        return pl.pallas_call(
            kernel,
            out_shape=shapes if single else list(shapes),
            compiler_params=params,
            cost_estimate=pl.CostEstimate(flops=flops, bytes_accessed=1 << 20, transcendentals=0),
            name=name,
            **more,
        )(*map(place, operands))

    loaded = (rhs, bases, transfer, codes)
    x, bases, transfer, codes = call(
        functools.partial(load_kernel, len(loaded)),
        [pltpu.VMEM(a.shape, a.dtype) for a in loaded],
        loaded,
        "load",
        place=outside,
        in_specs=[pl.BlockSpec(memory_space=pl.ANY)] * len(loaded),
        scratch_shapes=[pltpu.SemaphoreType.DMA((len(loaded),))],
    )
    facing, away, own0, own1, own2 = call(
        up_kernel,
        [
            pltpu.VMEM((6 * rows, 2 * rank), BF),
            pltpu.VMEM((6 * rows, 2 * rank), BF),
            pltpu.VMEM((leaves // 2 * rows, 2 * rank), BF),
            pltpu.VMEM((leaves // 4 * rows, 2 * rank), BF),
            pltpu.VMEM((rows, 2 * rank), BF),
        ],
        (x, bases, transfer),
        "up_sweep",
        1 << 32,
    )

    facing = exchanged(facing, 1)
    away = across_pairs(away)

    lifts = [pltpu.VMEM(((2 << k) * 2 * rank, 2 * rank), BF) for k in range(min(levels - 1, 2))]
    state, spread, links, masks, *lifts = call(
        functools.partial(plan_kernel, levels),
        [
            pltpu.VMEM((rows, leaves * rank), F32),
            pltpu.VMEM((5 * rank, leaves * rank), BF),
            pltpu.VMEM((levels * 4 * rank, 2 * rank), BF),
            pltpu.VMEM((8 * (levels + 1), 4 * rank), F32),
            *lifts,
        ],
        (facing, away, own0, own1, own2, codes, transfer, couple),
        "plan",
        1 << 30,
    )
    near = call(
        near_kernel,
        pltpu.VMEM((rows, leaves * size), F32),
        (facing, away, x, near_blocks),
        "near_field",
        3 * leaves * rows * size * size * 2,
    )

    received = []
    gathered = own2
    for group in stages[:-1]:
        got = [exchanged(gathered, m) for m in group]
        received.append(got)
        if group is not stages[-2]:
            gathered = stack(gathered, *got)
    parts = (gathered, *(received[-1] if received else ()))
    pay = call(
        pack_kernel,
        pltpu.VMEM((sum(part.shape[0] for part in parts), 2 * rank), BF),
        (masks, *parts),
        "pack",
    )
    received.append([exchanged(pay, 1)])

    flat = [g for got in received for g in got]
    return call(
        functools.partial(down_kernel, devices, stages, levels),
        jax.ShapeDtypeStruct((rows, leaves * size), BF),
        (own2, *flat, *lifts, state, spread, links, masks, transfer, bases, near),
        "down_sweep",
        scratch_shapes=[pltpu.VMEM((devices, rows, 2 * rank), BF)]
        + [pltpu.VMEM((devices >> k, rows, rank), F32) for k in range(levels)],
    )


def solution(mesh):
    return jax.shard_map(
        shards,
        mesh=mesh,
        in_specs=(
            P(None, ("groups", "leaf", "sub")),
            P(("groups", "leaf", "sub"), None, None),
            P(("groups", "leaf", "sub"), None, None, None),
            P(),
            P(),
            P(),
        ),
        out_specs=P(None, ("groups", "leaf", "sub")),
        check_vma=False,
    )
```

```python
import functools

import jax
import jax.numpy as jnp
from jax import lax
from jax.experimental import pallas as pl
from jax.experimental.pallas import tpu as pltpu
from jax.sharding import PartitionSpec as P

ROOT_HALF = 0.7071067811865476
OFFSETS = (-3, -2, 2, 3)
AXES = ("leaf", "sub")
BF = jnp.bfloat16
F32 = jnp.float32
LANES = 64


def mm(a, b):
    return lax.dot_general(a, b, (((1,), (0,)), ((), ())), preferred_element_type=F32)


def mm_t(a, b):
    return lax.dot_general(a, b, (((1,), (1,)), ((), ())), preferred_element_type=F32)


def split(a):
    high = a.astype(BF)
    low = (a - high.astype(F32)).astype(BF)
    return jnp.concatenate([high, low], axis=0)


def mm2(a, b, product=mm):
    out = product(split(a), b)
    return out[: a.shape[0]] + out[a.shape[0] :]


def halves(a, axis):
    high = a.astype(BF)
    return jnp.concatenate([high, (a - high.astype(F32)).astype(BF)], axis=axis)


def side(*parts):
    return jnp.concatenate(parts, axis=1)


def stack(*parts):
    return jnp.concatenate(parts, axis=0)


def stages_of(devices):
    bits = [1 << b for b in range(1, devices.bit_length() - 1)]
    rounds = [(bits.pop() | 1,)] if len(bits) % 2 else []
    while bits:
        high, low = bits.pop(), bits.pop()
        rounds.append((low | 1, high | 1, low | high))
    return rounds + [(1,)]


def slots_of(stages):
    held = [[0]]
    for masks in stages:
        so_far = [slot for part in held for slot in part]
        held += [[slot ^ m for slot in so_far] for m in masks]
    return held


def exchanged(x, apart):
    devices = lax.axis_size(AXES)
    return lax.ppermute(x, AXES, [(i, i ^ apart) for i in range(devices)])


def across_pairs(x):
    groups, devices = lax.axis_size("groups"), lax.axis_size(AXES)
    pairs = []
    for g in range(groups):
        for i in range(devices):
            j = i + 1 if i % 2 else i - 1
            to = (g, j) if 0 <= j < devices else ((g + 1) % groups, i)
            pairs.append((g * devices + i, to[0] * devices + to[1]))
    return lax.ppermute(x, ("groups", *AXES), pairs)


def first_kernel(rhs_hbm, bases_hbm, transfer_hbm, x, bases, low, leaf_coef, own2, sems):
    leaves, rank, size = bases.shape
    rows = x.shape[0]
    pairs = (
        (transfer_hbm.at[pl.ds(0, 2)], low),
        (bases_hbm, bases),
        (rhs_hbm, x),
    )
    copies = [pltpu.make_async_copy(*pair, sems.at[i]) for i, pair in enumerate(pairs)]
    for copy in copies:
        copy.start()
    copies[0].wait()
    table = low[0].reshape(2 * rank, rank)
    product = halves(stack(mm(table, low[1, 0]), mm(table, low[1, 1])) * (ROOT_HALF * ROOT_HALF), 1)
    copies[1].wait()
    copies[2].wait()
    at = lambda i: x[:, i * size : (i + 1) * size]
    first = lax.broadcasted_iota(jnp.int32, (rows, 2 * rank), 1) < rank
    parts = []
    for i in range(0, leaves, 2):
        both = mm_t(stack(at(i), at(i + 1)), bases[i : i + 2].reshape(2 * rank, size))
        parts.append(jnp.where(first, both[:rows], both[rows:]))
    leaf_coef[...] = stack(*parts)
    fours = stack(*[side(parts[i], parts[i + 1]) for i in range(0, leaves // 2, 2)])
    up = mm(halves(fours, 0), product)
    count = fours.shape[0]
    up = up[:count, :rank] + up[:count, rank:] + up[count:, :rank]
    own2[...] = side(*[up[i : i + rows] for i in range(0, count, rows)]).astype(BF)


def edges_kernel(leaf_coef, low, x, u2, facing, away, own0, own1):
    rank = low.shape[-1]
    rows = x.shape[0]
    own0[...] = leaf_coef[...].astype(BF)
    up1 = mm2(leaf_coef[...], low[0].reshape(2 * rank, rank)) * ROOT_HALF
    up1 = [up1[i : i + rows] for i in range(0, up1.shape[0], rows)]
    own1[...] = stack(*[side(up1[i], up1[i + 1]) for i in range(0, len(up1), 2)]).astype(BF)
    end = x.shape[1]
    size = end // (2 * len(up1))
    half = size // 2
    last0, last1 = own0.shape[0] - rows, own1.shape[0] - rows
    right = stack(
        x[:, end - size : end - half],
        x[:, end - half :],
        own0[last0:],
        own1[last1:],
        side(own0[last0 - rows : last0, rank:], own1[last1 - rows : last1, rank:]),
        u2[...],
    )
    left = stack(
        x[:, :half],
        x[:, half:size],
        own0[:rows],
        own1[:rows],
        side(own0[rows : 2 * rows, :rank], own1[rows : 2 * rows, :rank]),
        u2[...],
    )
    even = lax.axis_index(AXES) % 2 == 0
    facing[...] = jnp.where(even, right, left)
    away[...] = jnp.where(even, left, right)


def pack_kernel(after, *refs):
    *parts, out = refs
    at = 0
    for part in parts:
        out[at : at + part.shape[0]] = part[...]
        at += part.shape[0]


def mask_of(codes, level, leaves):
    p = lax.axis_index(AXES)
    wide = codes.shape[2]
    lanes = lax.broadcasted_iota(jnp.int32, (8, 4 * LANES), 1) // LANES
    offset = jnp.where(lanes < 2, lanes - 3, lanes)
    cluster = lax.broadcasted_iota(jnp.int32, (8, 4 * LANES), 0)
    diagonal = lax.broadcasted_iota(jnp.int32, (8, wide), 0) == lax.broadcasted_iota(jnp.int32, (8, wide), 1)
    count = leaves >> level
    index = p * count if count > 0 else p >> level - (leaves.bit_length() - 1)
    hit = jnp.zeros(lanes.shape, jnp.bool_)
    for slot in range(codes.shape[1]):
        row = jnp.broadcast_to(codes[level, slot : slot + 1], (8, wide))
        row = pltpu.roll(row, lax.rem(wide - index, wide), 1)
        code = jnp.sum(jnp.where(diagonal, row, 0).astype(F32), axis=1, keepdims=True)
        hit = hit | (lanes.astype(F32) == code)
    partner = index + cluster + offset
    hit = hit & (partner >= 0) & (partner < wide >> level)
    return jnp.where(hit, 1.0, 0.0)


def lowered(value, table, size):
    rank = value.shape[1]
    out = mm2(value, table, mm_t)
    parts = [out[i : i + size, j : j + rank] for i in range(0, out.shape[0], size) for j in (0, rank)]
    return stack(*parts)


def plan_kernel(facing, away, own0, own1, codes, transfer, couple, state, spread, links_out, masks, *lifts):
    rank = transfer.shape[-1]
    levels = masks.shape[0] // 8 - 3
    leaves = spread.shape[1] // rank
    p = lax.axis_index(AXES)
    table = lambda level: transfer[level].reshape(2 * rank, rank)
    beside = lambda rows: side(*[rows[i : i + rank] for i in range(0, rows.shape[0], rank)])

    mask = [mask_of(codes, level, leaves) for level in range(3 + levels)]
    masks[...] = stack(*mask)
    state[...] = couplings(facing, away, own0, own1, mask, transfer, couple)

    both = stack(transfer[2, 0].astype(F32).T, transfer[2, 1].astype(F32).T, couple[2, 0].astype(F32), couple[2, 3].astype(F32))
    both = beside(lowered(lowered(both, table(1), rank), table(0), rank))
    wide = leaves * rank
    high = both[:, :wide].astype(BF)
    spread[:rank] = high
    spread[rank : 2 * rank] = high
    spread[2 * rank : 3 * rank] = (both[:, :wide] - high.astype(F32)).astype(BF)
    first, second = both[:, wide : wide * 3 // 2].astype(BF), both[:, wide * 3 // 2 :].astype(BF)
    none = jnp.zeros_like(first)
    spread[3 * rank : 4 * rank] = side(first, none)
    spread[4 * rank :] = side(none, second)

    for k in range(levels):
        value = couple[3 + k].reshape(4 * rank, rank).astype(F32)
        for i in reversed(range(k)):
            value = mm2(value, transfer[3 + i, (p >> i) & 1], mm_t)
        links_out[4 * rank * k : 4 * rank * (k + 1)] = halves(value, 1)

    value = table(2).astype(F32) * ROOT_HALF
    for k, lift in enumerate(lifts):
        if k > 0:
            b = (p >> (k - 1)) & 1
            value = stack(*[mm2(value, transfer[2 + k, bit]) * ROOT_HALF for bit in (b, 1 - b)])
        lift[...] = halves(value, 1)


def sides_of(facing, away):
    p = lax.axis_index(AXES)
    even = p % 2 == 0
    away = jnp.where((p > 0) & (p < lax.axis_size(AXES) - 1), away, jnp.zeros_like(away))
    return jnp.where(even, away, facing), jnp.where(even, facing, away)


def near_kernel(facing, away, x, blocks, near):
    leaves, _, size, _ = blocks.shape
    rows = x.shape[0]
    left, right = sides_of(facing[: 2 * rows], away[: 2 * rows])
    before = side(left[:rows], left[rows:])
    after = side(right[:rows], right[rows:])
    at = lambda i: before if i < 0 else after if i == leaves else x[:, i * size : (i + 1) * size]
    for i in range(leaves):
        total = mm_t(at(i), blocks[i, 1])
        total += mm_t(at(i - 1), blocks[i, 0])
        total += mm_t(at(i + 1), blocks[i, 2])
        near[:, i * size : (i + 1) * size] = total


def couplings(facing, away, own0, own1, mask, transfer, couple):
    rank = transfer.shape[-1]
    leaves = mask[0].shape[0]
    rows = own0.shape[0] // leaves * 2
    table = lambda level: transfer[level].reshape(2 * rank, rank)
    left, right = sides_of(facing[...], away[...])
    block = lambda a, i: a[i * rows : (i + 1) * rows]
    lo = slice(0, rank)
    hi = slice(rank, 2 * rank)

    def coupled(level, ext, count):
        weights = mask[level].astype(BF)
        lhs = [side(*[ext[c + 3 + o] for o in OFFSETS]) * weights[c : c + 1] for c in range(count)]
        return mm(stack(*lhs), couple[level].reshape(4 * rank, rank))

    zero = jnp.zeros((rows, rank), BF)
    ext = [zero, block(left, 5)[:, lo], block(left, 5)[:, hi], zero, zero]
    ext += [block(right, 5)[:, lo], block(right, 5)[:, hi], zero]
    far2 = coupled(2, ext, 2)
    ext = [block(left, 4)[:, hi], block(left, 3)[:, lo], block(left, 3)[:, hi]]
    ext += [block(own1, c // 2)[:, (lo, hi)[c % 2]] for c in range(leaves // 2)]
    ext += [block(right, 3)[:, lo], block(right, 3)[:, hi], block(right, 4)[:, hi]]
    far1 = coupled(1, ext, leaves // 2)
    ext = [block(left, 4)[:, lo], block(left, 2)[:, lo], block(left, 2)[:, hi]]
    ext += [block(own0, c // 2)[:, (lo, hi)[c % 2]] for c in range(leaves)]
    ext += [block(right, 2)[:, lo], block(right, 2)[:, hi], block(right, 4)[:, lo]]
    far0 = coupled(0, ext, leaves)
    down = far0 + lowered(far1 + lowered(far2, table(1), rows), table(0), rows)
    return side(*[block(down, c) for c in range(leaves)])


def climb(up, count, transfer, level, bit, rows):
    rank = up.shape[1]
    pairs = up.reshape(count // 2, 2, rows, rank)
    children = [pairs[:, i].reshape(count // 2 * rows, rank) for i in range(2)]
    turned = stack(transfer[level, bit], transfer[level, 1 - bit])
    return mm2(side(*children), turned) * ROOT_HALF


def down_kernel(devices, stages, levels, *refs):
    refs = list(refs)
    slots = slots_of(stages)
    received = refs[: len(slots)]
    refs = refs[len(slots) :]
    lifts = [refs.pop(0) for _ in range(min(levels, 3))]
    state, spread, links, masks, transfer, bases, near, out, gathered, *ups = refs
    leaves, rank, size = bases.shape
    rows = out.shape[0]
    p = lax.axis_index(AXES)

    for part, ref in zip(slots, received):
        for i, slot in enumerate(part):
            gathered[slot] = ref[i * rows : (i + 1) * rows]

    def raised(k, first, count):
        sets = [side(*[gathered[first[i] + j] for j in range(1 << k)]) for i in range(count)]
        up = mm(stack(*sets), lifts[k][...])
        return up[:, :rank] + up[:, rank:]

    if ups:
        count = devices >> 2
        up = raised(2, [4 * i for i in range(count)], count)
        for k in range(3, levels):
            up = climb(up, count, transfer, 2 + k, (p >> (k - 1)) & 1, rows)
            count //= 2
            ups[k - 3][...] = up.reshape(count, rows, rank)
    lhs = []
    for k in range(levels):
        a = p >> k
        n = devices >> k
        places = [a ^ jnp.clip(a + o, 0, n - 1) for o in OFFSETS]
        if k < 3:
            up = raised(k, [place << k for place in places], 4)
            parts = [up[i * rows : (i + 1) * rows] for i in range(4)]
        else:
            parts = [ups[k - 3][place] for place in places]
        lhs.append(side(*parts) * masks[8 * (3 + k) : 8 * (3 + k) + 1])
    top = mm(halves(side(*lhs), 0), links[...])
    top = top[:rows, :rank] + top[:rows, rank:] + top[rows:, :rank] + top[rows:, rank:]

    at = lambda o: gathered[p ^ jnp.clip(p + o, 0, devices - 1)]
    weights = masks[16:24].astype(BF)
    before = at(-2)[:, rank:] * weights[0:1, :rank]
    after = at(2)[:, :rank] * weights[1:2, 3 * rank :]
    lhs = side(halves(top, 1), top.astype(BF), before, after)
    coef = (mm(lhs, spread[...]) + state[...]).astype(BF)
    for c in range(leaves):
        cols = slice(c * size, (c + 1) * size)
        out[:, cols] = (mm(coef[:, c * rank : (c + 1) * rank], bases[c]) + near[:, cols]).astype(BF)


def inside(x):
    return pltpu.with_memory_space_constraint(x, pltpu.VMEM)


def outside(x):
    return pltpu.with_memory_space_constraint(x, pltpu.HBM)


def shards(rhs, bases, near_blocks, transfer, couple, codes):
    rows = rhs.shape[0]
    leaves, rank, size = bases.shape
    devices = lax.axis_size(AXES)
    stages = stages_of(devices)
    levels = devices.bit_length() - 2
    params = pltpu.CompilerParams(vmem_limit_bytes=16 << 20)

    def call(kernel, shapes, operands, name, flops=0, place=inside, **more):
        single = not isinstance(shapes, list)
        return pl.pallas_call(
            kernel,
            out_shape=shapes if single else list(shapes),
            compiler_params=params,
            cost_estimate=pl.CostEstimate(flops=flops, bytes_accessed=1 << 20, transcendentals=0),
            name=name,
            **more,
        )(*map(place, operands))

    x, bases, low, leaf_coef, own2 = call(
        first_kernel,
        [
            pltpu.VMEM(rhs.shape, BF),
            pltpu.VMEM(bases.shape, BF),
            pltpu.VMEM((2, 2, rank, rank), BF),
            pltpu.VMEM((leaves // 2 * rows, 2 * rank), F32),
            pltpu.VMEM((rows, 2 * rank), BF),
        ],
        (rhs, bases, transfer),
        "first",
        1 << 32,
        place=outside,
        in_specs=[pl.BlockSpec(memory_space=pl.ANY)] * 3,
        scratch_shapes=[pltpu.SemaphoreType.DMA((3,))],
    )
    facing, away, own0, own1 = call(
        edges_kernel,
        [
            pltpu.VMEM((6 * rows, 2 * rank), BF),
            pltpu.VMEM((6 * rows, 2 * rank), BF),
            pltpu.VMEM((leaves // 2 * rows, 2 * rank), BF),
            pltpu.VMEM((leaves // 4 * rows, 2 * rank), BF),
        ],
        (leaf_coef, low, x, own2),
        "edges",
    )

    facing = exchanged(facing, 1)
    away = across_pairs(away)

    lifts = [pltpu.VMEM(((2 << k) * rank, 2 * rank), BF) for k in range(min(levels, 3))]
    state, spread, links, masks, *lifts = call(
        plan_kernel,
        [
            pltpu.VMEM((rows, leaves * rank), F32),
            pltpu.VMEM((5 * rank, leaves * rank), BF),
            pltpu.VMEM((levels * 4 * rank, 2 * rank), BF),
            pltpu.VMEM((8 * (3 + levels), 4 * rank), F32),
            *lifts,
        ],
        (facing, away, own0, own1, codes, transfer, couple),
        "plan",
        1 << 30,
    )

    gathered = own2
    received = [own2]
    for group in stages[:-1]:
        got = [exchanged(gathered, m) for m in group]
        received += got
        if group is not stages[-2]:
            gathered = stack(gathered, *got)
    parts = (gathered, *got) if len(stages) > 1 else (gathered,)
    pay = call(
        pack_kernel,
        pltpu.VMEM((sum(part.shape[0] for part in parts), 2 * rank), BF),
        (masks, *parts),
        "pack",
    )
    received.append(exchanged(pay, 1))

    near = call(
        near_kernel,
        pltpu.VMEM((rows, leaves * size), F32),
        (facing, away, x, near_blocks),
        "near_field",
        3 * leaves * rows * size * size * 2,
    )
    return call(
        functools.partial(down_kernel, devices, stages, levels),
        jax.ShapeDtypeStruct((rows, leaves * size), BF),
        (*received, *lifts, state, spread, links, masks, transfer, bases, near),
        "down_sweep",
        scratch_shapes=[pltpu.VMEM((devices, rows, 2 * rank), BF)]
        + [pltpu.VMEM((devices >> k, rows, rank), F32) for k in range(3, levels)],
    )


def solution(mesh):
    return jax.shard_map(
        shards,
        mesh=mesh,
        in_specs=(
            P(None, ("groups", "leaf", "sub")),
            P(("groups", "leaf", "sub"), None, None),
            P(("groups", "leaf", "sub"), None, None, None),
            P(),
            P(),
            P(),
        ),
        out_specs=P(None, ("groups", "leaf", "sub")),
        check_vma=False,
    )
```

```python
import functools

import jax
import jax.numpy as jnp
from jax import lax
from jax.experimental import pallas as pl
from jax.experimental.pallas import tpu as pltpu
from jax.sharding import PartitionSpec as P

ROOT_HALF = 0.7071067811865476
OFFSETS = (-3, -2, 2, 3)
AXES = ("leaf", "sub")
BF = jnp.bfloat16
F32 = jnp.float32
LANES = 64
SHARE = 2


def mm(a, b):
    return lax.dot_general(a, b, (((1,), (0,)), ((), ())), preferred_element_type=F32)


def mm_t(a, b):
    return lax.dot_general(a, b, (((1,), (1,)), ((), ())), preferred_element_type=F32)


def split(a):
    high = a.astype(BF)
    low = (a - high.astype(F32)).astype(BF)
    return jnp.concatenate([high, low], axis=0)


def mm2(a, b, product=mm):
    out = product(split(a), b)
    return out[: a.shape[0]] + out[a.shape[0] :]


def halves(a, axis):
    high = a.astype(BF)
    return jnp.concatenate([high, (a - high.astype(F32)).astype(BF)], axis=axis)


def side(*parts):
    return jnp.concatenate(parts, axis=1)


def stack(*parts):
    return jnp.concatenate(parts, axis=0)


def stages_of(devices):
    bits = [1 << b for b in range(1, devices.bit_length() - 1)]
    rounds = [(bits.pop() | 1,)] if len(bits) % 2 else []
    while bits:
        high, low = bits.pop(), bits.pop()
        rounds.append((low | 1, high | 1, low | high))
    return rounds + [(1,)]


def slots_of(stages):
    held = [[0]]
    for masks in stages:
        so_far = [slot for part in held for slot in part]
        held += [[slot ^ m for slot in so_far] for m in masks]
    return held


def exchanged(x, apart):
    devices = lax.axis_size(AXES)
    return lax.ppermute(x, AXES, [(i, i ^ apart) for i in range(devices)])


def across_pairs(x):
    groups, devices = lax.axis_size("groups"), lax.axis_size(AXES)
    pairs = []
    for g in range(groups):
        for i in range(devices):
            j = i + 1 if i % 2 else i - 1
            to = (g, j) if 0 <= j < devices else ((g + 1) % groups, i)
            pairs.append((g * devices + i, to[0] * devices + to[1]))
    return lax.ppermute(x, ("groups", *AXES), pairs)


def first_kernel(rhs_hbm, bases_hbm, transfer_hbm, x, bases, facing, away, own0, own1, own2, low, sems):
    leaves, rank, size = bases.shape
    rows = x.shape[0]
    pairs = (
        (transfer_hbm.at[pl.ds(0, 2)], low),
        (bases_hbm, bases),
        (rhs_hbm, x),
    )
    copies = [pltpu.make_async_copy(*pair, sems.at[i]) for i, pair in enumerate(pairs)]
    for copy in copies:
        copy.start()
    copies[0].wait()
    table = low[0].reshape(2 * rank, rank)
    product = halves(stack(mm(table, low[1, 0]), mm(table, low[1, 1])) * (ROOT_HALF * ROOT_HALF), 1)
    copies[1].wait()
    copies[2].wait()
    at = lambda i: x[:, i * size : (i + 1) * size]
    first = lax.broadcasted_iota(jnp.int32, (rows, 2 * rank), 1) < rank
    parts = []
    for i in range(0, leaves, 2):
        both = mm_t(stack(at(i), at(i + 1)), bases[i : i + 2].reshape(2 * rank, size))
        parts.append(jnp.where(first, both[:rows], both[rows:]))
    leaf_coef = stack(*parts)
    fours = stack(*[side(parts[i], parts[i + 1]) for i in range(0, leaves // 2, 2)])
    up = mm(halves(fours, 0), product)
    count = fours.shape[0]
    up = up[:count, :rank] + up[:count, rank:] + up[count:, :rank]
    own2[...] = side(*[up[i : i + rows] for i in range(0, count, rows)]).astype(BF)
    u2 = own2

    own0[...] = leaf_coef.astype(BF)
    up1 = mm2(leaf_coef, table) * ROOT_HALF
    up1 = [up1[i : i + rows] for i in range(0, up1.shape[0], rows)]
    own1[...] = stack(*[side(up1[i], up1[i + 1]) for i in range(0, len(up1), 2)]).astype(BF)
    end = x.shape[1]
    half = size // 2
    last0, last1 = own0.shape[0] - rows, own1.shape[0] - rows
    right = stack(
        x[:, end - size : end - half],
        x[:, end - half :],
        own0[last0:],
        own1[last1:],
        side(own0[last0 - rows : last0, rank:], own1[last1 - rows : last1, rank:]),
        u2[...],
    )
    left = stack(
        x[:, :half],
        x[:, half:size],
        own0[:rows],
        own1[:rows],
        side(own0[rows : 2 * rows, :rank], own1[rows : 2 * rows, :rank]),
        u2[...],
    )
    even = lax.axis_index(AXES) % 2 == 0
    facing[...] = jnp.where(even, right, left)
    away[...] = jnp.where(even, left, right)


def pack_kernel(after, *refs):
    *parts, out = refs
    at = 0
    for part in parts:
        out[at : at + part.shape[0]] = part[...]
        at += part.shape[0]


def mask_of(codes, level, leaves, p):
    wide = codes.shape[2]
    lanes = lax.broadcasted_iota(jnp.int32, (8, 4 * LANES), 1) // LANES
    offset = jnp.where(lanes < 2, lanes - 3, lanes)
    cluster = lax.broadcasted_iota(jnp.int32, (8, 4 * LANES), 0)
    diagonal = lax.broadcasted_iota(jnp.int32, (8, wide), 0) == lax.broadcasted_iota(jnp.int32, (8, wide), 1)
    count = leaves >> level
    index = p * count if count > 0 else p >> level - (leaves.bit_length() - 1)
    hit = jnp.zeros(lanes.shape, jnp.bool_)
    for slot in range(codes.shape[1]):
        row = jnp.broadcast_to(codes[level, slot : slot + 1], (8, wide))
        row = pltpu.roll(row, lax.rem(wide - index, wide), 1)
        code = jnp.sum(jnp.where(diagonal, row, 0).astype(F32), axis=1, keepdims=True)
        hit = hit | (lanes.astype(F32) == code)
    partner = index + cluster + offset
    hit = hit & (partner >= 0) & (partner < wide >> level)
    return jnp.where(hit, 1.0, 0.0)


def lowered(value, table, size):
    rank = value.shape[1]
    out = mm2(value, table, mm_t)
    parts = [out[i : i + size, j : j + rank] for i in range(0, out.shape[0], size) for j in (0, rank)]
    return stack(*parts)


def spread_tables(transfer, couple, spread):
    rank = transfer.shape[-1]
    leaves = spread.shape[1] // rank
    table = lambda level: transfer[level].reshape(2 * rank, rank)
    beside = lambda rows: side(*[rows[i : i + rank] for i in range(0, rows.shape[0], rank)])
    both = stack(transfer[2, 0].astype(F32).T, transfer[2, 1].astype(F32).T, couple[2, 0].astype(F32), couple[2, 3].astype(F32))
    both = beside(lowered(lowered(both, table(1), rank), table(0), rank))
    wide = leaves * rank
    high = both[:, :wide].astype(BF)
    spread[:rank] = high
    spread[rank : 2 * rank] = high
    spread[2 * rank : 3 * rank] = (both[:, :wide] - high.astype(F32)).astype(BF)
    first, second = both[:, wide : wide * 3 // 2].astype(BF), both[:, wide * 3 // 2 :].astype(BF)
    none = jnp.zeros_like(first)
    spread[3 * rank : 4 * rank] = side(first, none)
    spread[4 * rank :] = side(none, second)


def plan_kernel(facing, away, own0, own1, codes, transfer, couple, state, spread, links_out, masks, *lifts):
    rank = transfer.shape[-1]
    levels = masks.shape[0] // 8 - 3
    leaves = spread.shape[1] // rank
    p = lax.axis_index(AXES)
    table = lambda level: transfer[level].reshape(2 * rank, rank)

    mask = [mask_of(codes, level, leaves, p) for level in range(3 + levels)]
    masks[...] = stack(*mask)
    state[...] = couplings(facing, away, own0, own1, mask, transfer, couple)
    spread_tables(transfer, couple, spread)

    for k in range(levels):
        value = couple[3 + k].reshape(4 * rank, rank).astype(F32)
        for i in reversed(range(k)):
            value = mm2(value, transfer[3 + i, (p >> i) & 1], mm_t)
        links_out[4 * rank * k : 4 * rank * (k + 1)] = halves(value, 1)

    value = table(2).astype(F32) * ROOT_HALF
    for k, lift in enumerate(lifts):
        if k > 0:
            b = (p >> (k - 1)) & 1
            value = stack(*[mm2(value, transfer[2 + k, bit]) * ROOT_HALF for bit in (b, 1 - b)])
        lift[...] = halves(value, 1)


def sides_of(facing, away):
    p = lax.axis_index(AXES)
    even = p % 2 == 0
    away = jnp.where((p > 0) & (p < lax.axis_size(AXES) - 1), away, jnp.zeros_like(away))
    return jnp.where(even, away, facing), jnp.where(even, facing, away)


def near_kernel(first, facing, away, x, blocks, near):
    _, _, size, _ = blocks.shape
    leaves = x.shape[1] // size
    rows = x.shape[0]
    left, right = sides_of(facing[: 2 * rows], away[: 2 * rows])
    before = side(left[:rows], left[rows:])
    after = side(right[:rows], right[rows:])
    at = lambda i: before if i < 0 else after if i == leaves else x[:, i * size : (i + 1) * size]
    for i in range(first, first + near.shape[1] // size):
        total = mm_t(at(i), blocks[i, 1])
        total += mm_t(at(i - 1), blocks[i, 0])
        total += mm_t(at(i + 1), blocks[i, 2])
        near[:, (i - first) * size : (i - first + 1) * size] = total


def couplings(facing, away, own0, own1, mask, transfer, couple):
    rank = transfer.shape[-1]
    leaves = mask[0].shape[0]
    rows = own0.shape[0] // leaves * 2
    table = lambda level: transfer[level].reshape(2 * rank, rank)
    left, right = sides_of(facing[...], away[...])
    block = lambda a, i: a[i * rows : (i + 1) * rows]
    lo = slice(0, rank)
    hi = slice(rank, 2 * rank)

    def coupled(level, ext, count):
        weights = mask[level].astype(BF)
        lhs = [side(*[ext[c + 3 + o] for o in OFFSETS]) * weights[c : c + 1] for c in range(count)]
        return mm(stack(*lhs), couple[level].reshape(4 * rank, rank))

    zero = jnp.zeros((rows, rank), BF)
    ext = [zero, block(left, 5)[:, lo], block(left, 5)[:, hi], zero, zero]
    ext += [block(right, 5)[:, lo], block(right, 5)[:, hi], zero]
    far2 = coupled(2, ext, 2)
    ext = [block(left, 4)[:, hi], block(left, 3)[:, lo], block(left, 3)[:, hi]]
    ext += [block(own1, c // 2)[:, (lo, hi)[c % 2]] for c in range(leaves // 2)]
    ext += [block(right, 3)[:, lo], block(right, 3)[:, hi], block(right, 4)[:, hi]]
    far1 = coupled(1, ext, leaves // 2)
    ext = [block(left, 4)[:, lo], block(left, 2)[:, lo], block(left, 2)[:, hi]]
    ext += [block(own0, c // 2)[:, (lo, hi)[c % 2]] for c in range(leaves)]
    ext += [block(right, 2)[:, lo], block(right, 2)[:, hi], block(right, 4)[:, lo]]
    far0 = coupled(0, ext, leaves)
    down = far0 + lowered(far1 + lowered(far2, table(1), rows), table(0), rows)
    return side(*[block(down, c) for c in range(leaves)])


def dense_plan_kernel(
    levels, slots, facing, away, own0, own1, codes, transfer, couple, state, spread, masks, weights, chosen
):
    rank = transfer.shape[-1]
    leaves = spread.shape[1] // rank
    p = lax.axis_index(AXES)

    mask = [mask_of(codes, level, leaves, p) for level in range(3)]
    masks[:8] = mask[2]
    masks[8:] = mask_of(codes, 2, leaves, p ^ 1)
    state[...] = couplings(facing, away, own0, own1, mask, transfer, couple)
    spread_tables(transfer, couple, spread)

    for k in range(levels):
        value = couple[3 + k].reshape(4 * rank, rank).astype(F32)
        for i in reversed(range(1, k)):
            value = mm2(value, transfer[3 + i, (p >> i) & 1], mm_t)
        for j in range(2):
            device = p ^ j
            low = mm2(value, transfer[3, device & 1], mm_t) if k > 0 else value
            hit = mask_of(codes, 3 + k, leaves, device)
            for q in range(4):
                part = low[q * rank : (q + 1) * rank] * hit[:1, q * rank : (q + 1) * rank]
                chosen[2 * k + j, q] = part.astype(BF)
            chosen[2 * k + j, 4] = jnp.zeros((rank, rank), BF)

    lifts = [[transfer[2].reshape(2 * rank, rank).astype(F32) * ROOT_HALF]]
    for k in range(1, levels):
        b = (p >> (k - 1)) & 1
        lifts.append([mm2(a, transfer[2 + k, bit]) * ROOT_HALF for bit in (b, 1 - b) for a in lifts[-1]])
    lifts = [[halves(a, 0) for a in level] for level in lifts]

    for i, slot in enumerate(slots):
        picked = []
        for k in range(levels):
            both = []
            for j in range(2):
                apart = ((p ^ slot) >> k) - ((p ^ j) >> k)
                q = jnp.where(apart < 0, apart + 3, apart)
                q = jnp.where((apart >= -3) & (apart <= 3) & (apart * apart >= 4), q, 4)
                both.append(chosen[2 * k + j, q])
            picked.append(side(*both))
        lift = side(*[lifts[k][slot & ((1 << k) - 1)] for k in range(levels)])
        out = mm(lift, stack(*picked))
        weights[2 * rank * i : 2 * rank * (i + 1)] = (out[: 2 * rank] + out[2 * rank :]).astype(BF)


def half_kernel(devices, slots, waits, masks, weights, *refs):
    *parts, mine, theirs, gathered = refs
    parts = parts[: len(parts) - waits]
    rank = weights.shape[1] // 2
    rows = mine.shape[0]
    p = lax.axis_index(AXES)
    gathered[...] = jnp.zeros(gathered.shape, BF)
    found = [part[i : i + rows] for part in parts for i in range(0, part.shape[0], rows)]
    for slot, value in zip(slots, found):
        gathered[slot] = value
    top = mm(side(*found), weights[...])
    for j, out in ((0, mine), (1, theirs)):
        device = p ^ j
        at = lambda o: gathered[p ^ jnp.clip(device + o, 0, devices - 1)]
        hit = masks[8 * j : 8 * j + 8].astype(BF)
        before = at(-2)[:, rank:] * hit[0:1, :rank]
        after = at(2)[:, :rank] * hit[1:2, 3 * rank :]
        out[...] = side(halves(top[:, j * rank : (j + 1) * rank], 1), before, after)


def leaves_kernel(count, mine, theirs, state, spread, bases, *refs):
    out = refs[-1]
    leaves, rank, size = bases.shape
    near = [(ref, i) for ref in refs[:count] for i in range(0, ref.shape[1], size)]
    a, b = mine[...].astype(F32), theirs[...].astype(F32)
    top = (a[:, :rank] + b[:, :rank]) + (a[:, rank : 2 * rank] + b[:, rank : 2 * rank])
    lhs = side(halves(top, 1), top.astype(BF), (a[:, 2 * rank :] + b[:, 2 * rank :]).astype(BF))
    coef = (mm(lhs, spread[...]) + state[...]).astype(BF)
    for c in range(leaves):
        ref, at = near[c]
        total = mm(coef[:, c * rank : (c + 1) * rank], bases[c]) + ref[:, at : at + size]
        out[:, c * size : (c + 1) * size] = total.astype(BF)


def climb(up, count, transfer, level, bit, rows):
    rank = up.shape[1]
    pairs = up.reshape(count // 2, 2, rows, rank)
    children = [pairs[:, i].reshape(count // 2 * rows, rank) for i in range(2)]
    turned = stack(transfer[level, bit], transfer[level, 1 - bit])
    return mm2(side(*children), turned) * ROOT_HALF


def down_kernel(devices, stages, levels, *refs):
    refs = list(refs)
    slots = slots_of(stages)
    received = refs[: len(slots)]
    refs = refs[len(slots) :]
    lifts = [refs.pop(0) for _ in range(min(levels, 3))]
    state, spread, links, masks, transfer, bases, near, out, gathered, *ups = refs
    leaves, rank, size = bases.shape
    rows = out.shape[0]
    p = lax.axis_index(AXES)

    for part, ref in zip(slots, received):
        for i, slot in enumerate(part):
            gathered[slot] = ref[i * rows : (i + 1) * rows]

    def raised(k, first, count):
        sets = [side(*[gathered[first[i] + j] for j in range(1 << k)]) for i in range(count)]
        up = mm(stack(*sets), lifts[k][...])
        return up[:, :rank] + up[:, rank:]

    if ups:
        count = devices >> 2
        up = raised(2, [4 * i for i in range(count)], count)
        for k in range(3, levels):
            up = climb(up, count, transfer, 2 + k, (p >> (k - 1)) & 1, rows)
            count //= 2
            ups[k - 3][...] = up.reshape(count, rows, rank)
    lhs = []
    for k in range(levels):
        a = p >> k
        n = devices >> k
        places = [a ^ jnp.clip(a + o, 0, n - 1) for o in OFFSETS]
        if k < 3:
            up = raised(k, [place << k for place in places], 4)
            parts = [up[i * rows : (i + 1) * rows] for i in range(4)]
        else:
            parts = [ups[k - 3][place] for place in places]
        lhs.append(side(*parts) * masks[8 * (3 + k) : 8 * (3 + k) + 1])
    top = mm(halves(side(*lhs), 0), links[...])
    top = top[:rows, :rank] + top[:rows, rank:] + top[rows:, :rank] + top[rows:, rank:]

    at = lambda o: gathered[p ^ jnp.clip(p + o, 0, devices - 1)]
    weights = masks[16:24].astype(BF)
    before = at(-2)[:, rank:] * weights[0:1, :rank]
    after = at(2)[:, :rank] * weights[1:2, 3 * rank :]
    lhs = side(halves(top, 1), top.astype(BF), before, after)
    coef = (mm(lhs, spread[...]) + state[...]).astype(BF)
    for c in range(leaves):
        cols = slice(c * size, (c + 1) * size)
        out[:, cols] = (mm(coef[:, c * rank : (c + 1) * rank], bases[c]) + near[:, cols]).astype(BF)


def inside(x):
    return pltpu.with_memory_space_constraint(x, pltpu.VMEM)


def outside(x):
    return pltpu.with_memory_space_constraint(x, pltpu.HBM)


def shards(rhs, bases, near_blocks, transfer, couple, codes):
    rows = rhs.shape[0]
    leaves, rank, size = bases.shape
    devices = lax.axis_size(AXES)
    stages = stages_of(devices)
    levels = devices.bit_length() - 2
    params = pltpu.CompilerParams(vmem_limit_bytes=16 << 20)

    def call(kernel, shapes, operands, name, flops=0, place=inside, **more):
        single = not isinstance(shapes, list)
        return pl.pallas_call(
            kernel,
            out_shape=shapes if single else list(shapes),
            compiler_params=params,
            cost_estimate=pl.CostEstimate(flops=flops, bytes_accessed=1 << 20, transcendentals=0),
            name=name,
            **more,
        )(*map(place, operands))

    x, bases, facing, away, own0, own1, own2 = call(
        first_kernel,
        [
            pltpu.VMEM(rhs.shape, BF),
            pltpu.VMEM(bases.shape, BF),
            pltpu.VMEM((6 * rows, 2 * rank), BF),
            pltpu.VMEM((6 * rows, 2 * rank), BF),
            pltpu.VMEM((leaves // 2 * rows, 2 * rank), BF),
            pltpu.VMEM((leaves // 4 * rows, 2 * rank), BF),
            pltpu.VMEM((rows, 2 * rank), BF),
        ],
        (rhs, bases, transfer),
        "first",
        1 << 32,
        place=outside,
        in_specs=[pl.BlockSpec(memory_space=pl.ANY)] * 3,
        scratch_shapes=[pltpu.VMEM((2, 2, rank, rank), BF), pltpu.SemaphoreType.DMA((3,))],
    )

    facing = exchanged(facing, 1)
    away = across_pairs(away)

    dense = levels <= 3
    if dense:
        slots = [slot for part in slots_of(stages)[:-1] for slot in part]
        state, spread, masks, weights = call(
            functools.partial(dense_plan_kernel, levels, slots),
            [
                pltpu.VMEM((rows, leaves * rank), F32),
                pltpu.VMEM((5 * rank, leaves * rank), BF),
                pltpu.VMEM((16, 4 * rank), F32),
                pltpu.VMEM((2 * rank * len(slots), 2 * rank), BF),
            ],
            (facing, away, own0, own1, codes, transfer, couple),
            "plan",
            1 << 30,
            scratch_shapes=[pltpu.VMEM((2 * levels, 5, rank, rank), BF)],
        )
    else:
        lifts = [pltpu.VMEM(((2 << k) * rank, 2 * rank), BF) for k in range(min(levels, 3))]
        state, spread, links, masks, *lifts = call(
            plan_kernel,
            [
                pltpu.VMEM((rows, leaves * rank), F32),
                pltpu.VMEM((5 * rank, leaves * rank), BF),
                pltpu.VMEM((levels * 4 * rank, 2 * rank), BF),
                pltpu.VMEM((8 * (3 + levels), 4 * rank), F32),
                *lifts,
            ],
            (facing, away, own0, own1, codes, transfer, couple),
            "plan",
            1 << 30,
        )

    def near_of(first, count):
        return call(
            functools.partial(near_kernel, first),
            pltpu.VMEM((rows, count * size), F32),
            (facing, away, x, near_blocks),
            "near_field",
            3 * count * rows * size * size * 2,
        )

    some = leaves * SHARE // 8 if dense else 0
    near = (near_of(0, some),) if some else ()
    gathered = own2
    received = [own2]
    for group in stages[:-1]:
        got = [exchanged(gathered, m) for m in group]
        received += got
        if group is not stages[-2]:
            gathered = stack(gathered, *got)
    if dense:
        mine, theirs = call(
            functools.partial(half_kernel, devices, slots, len(near)),
            [pltpu.VMEM((rows, 4 * rank), BF), pltpu.VMEM((rows, 4 * rank), BF)],
            (masks, weights, *received, *near),
            "half",
            scratch_shapes=[pltpu.VMEM((devices, rows, 2 * rank), BF)],
        )
        theirs = exchanged(theirs, 1)
    else:
        parts = (gathered, *got) if len(stages) > 1 else (gathered,)
        pay = call(
            pack_kernel,
            pltpu.VMEM((sum(part.shape[0] for part in parts), 2 * rank), BF),
            (masks, *parts),
            "pack",
        )
        received.append(exchanged(pay, 1))

    near = (*near, near_of(some, leaves - some))
    if dense:
        return call(
            functools.partial(leaves_kernel, len(near)),
            jax.ShapeDtypeStruct((rows, leaves * size), BF),
            (mine, theirs, state, spread, bases, *near, *received, masks, weights, transfer),
            "leaves",
        )
    return call(
        functools.partial(down_kernel, devices, stages, levels),
        jax.ShapeDtypeStruct((rows, leaves * size), BF),
        (*received, *lifts, state, spread, links, masks, transfer, bases, *near),
        "down_sweep",
        scratch_shapes=[pltpu.VMEM((devices, rows, 2 * rank), BF)]
        + [pltpu.VMEM((devices >> k, rows, rank), F32) for k in range(3, levels)],
    )


def solution(mesh):
    return jax.shard_map(
        shards,
        mesh=mesh,
        in_specs=(
            P(None, ("groups", "leaf", "sub")),
            P(("groups", "leaf", "sub"), None, None),
            P(("groups", "leaf", "sub"), None, None, None),
            P(),
            P(),
            P(),
        ),
        out_specs=P(None, ("groups", "leaf", "sub")),
        check_vma=False,
    )
```

```python
import functools

import jax
import jax.numpy as jnp
from jax import lax
from jax.experimental import pallas as pl
from jax.experimental.pallas import tpu as pltpu
from jax.sharding import PartitionSpec as P

ROOT_HALF = 0.7071067811865476
OFFSETS = (-3, -2, 2, 3)
AXES = ("leaf", "sub")
BF = jnp.bfloat16
F32 = jnp.float32
LANES = 64
SHARE = 2


def mm(a, b):
    return lax.dot_general(a, b, (((1,), (0,)), ((), ())), preferred_element_type=F32)


def mm_t(a, b):
    return lax.dot_general(a, b, (((1,), (1,)), ((), ())), preferred_element_type=F32)


def split(a):
    high = a.astype(BF)
    low = (a - high.astype(F32)).astype(BF)
    return jnp.concatenate([high, low], axis=0)


def mm2(a, b, product=mm):
    out = product(split(a), b)
    return out[: a.shape[0]] + out[a.shape[0] :]


def halves(a, axis):
    high = a.astype(BF)
    return jnp.concatenate([high, (a - high.astype(F32)).astype(BF)], axis=axis)


def side(*parts):
    return jnp.concatenate(parts, axis=1)


def stack(*parts):
    return jnp.concatenate(parts, axis=0)


def stages_of(devices):
    bits = [1 << b for b in range(1, devices.bit_length() - 1)]
    rounds = [(bits.pop() | 1,)] if len(bits) % 2 else []
    while bits:
        high, low = bits.pop(), bits.pop()
        rounds.append((low | 1, high | 1, low | high))
    return rounds + [(1,)]


def slots_of(stages):
    held = [[0]]
    for masks in stages:
        so_far = [slot for part in held for slot in part]
        held += [[slot ^ m for slot in so_far] for m in masks]
    return held


def exchanged(x, apart):
    devices = lax.axis_size(AXES)
    return lax.ppermute(x, AXES, [(i, i ^ apart) for i in range(devices)])


def across_pairs(x):
    groups, devices = lax.axis_size("groups"), lax.axis_size(AXES)
    pairs = []
    for g in range(groups):
        for i in range(devices):
            j = i + 1 if i % 2 else i - 1
            to = (g, j) if 0 <= j < devices else ((g + 1) % groups, i)
            pairs.append((g * devices + i, to[0] * devices + to[1]))
    return lax.ppermute(x, ("groups", *AXES), pairs)


def first_kernel(rhs_hbm, bases_hbm, transfer_hbm, x, bases, facing, away, own0, own1, own2, low, sems):
    leaves, rank, size = bases.shape
    rows = x.shape[0]
    pairs = (
        (transfer_hbm.at[pl.ds(0, 2)], low),
        (bases_hbm, bases),
        (rhs_hbm, x),
    )
    copies = [pltpu.make_async_copy(*pair, sems.at[i]) for i, pair in enumerate(pairs)]
    for copy in copies:
        copy.start()
    copies[0].wait()
    table = low[0].reshape(2 * rank, rank)
    product = halves(stack(mm(table, low[1, 0]), mm(table, low[1, 1])) * (ROOT_HALF * ROOT_HALF), 1)
    copies[1].wait()
    copies[2].wait()
    at = lambda i: x[:, i * size : (i + 1) * size]
    first = lax.broadcasted_iota(jnp.int32, (rows, 2 * rank), 1) < rank
    parts = []
    for i in range(0, leaves, 2):
        both = mm_t(stack(at(i), at(i + 1)), bases[i : i + 2].reshape(2 * rank, size))
        parts.append(jnp.where(first, both[:rows], both[rows:]))
    leaf_coef = stack(*parts)
    fours = stack(*[side(parts[i], parts[i + 1]) for i in range(0, leaves // 2, 2)])
    up = mm(halves(fours, 0), product)
    count = fours.shape[0]
    up = up[:count, :rank] + up[:count, rank:] + up[count:, :rank]
    own2[...] = side(*[up[i : i + rows] for i in range(0, count, rows)]).astype(BF)
    u2 = own2

    own0[...] = leaf_coef.astype(BF)
    up1 = mm2(leaf_coef, table) * ROOT_HALF
    up1 = [up1[i : i + rows] for i in range(0, up1.shape[0], rows)]
    own1[...] = stack(*[side(up1[i], up1[i + 1]) for i in range(0, len(up1), 2)]).astype(BF)
    end = x.shape[1]
    half = size // 2
    last0, last1 = own0.shape[0] - rows, own1.shape[0] - rows
    right = stack(
        x[:, end - size : end - half],
        x[:, end - half :],
        own0[last0:],
        own1[last1:],
        side(own0[last0 - rows : last0, rank:], own1[last1 - rows : last1, rank:]),
        u2[...],
    )
    left = stack(
        x[:, :half],
        x[:, half:size],
        own0[:rows],
        own1[:rows],
        side(own0[rows : 2 * rows, :rank], own1[rows : 2 * rows, :rank]),
        u2[...],
    )
    even = lax.axis_index(AXES) % 2 == 0
    facing[...] = jnp.where(even, right, left)
    away[...] = jnp.where(even, left, right)


def pack_kernel(after, *refs):
    *parts, out = refs
    at = 0
    for part in parts:
        out[at : at + part.shape[0]] = part[...]
        at += part.shape[0]


def mask_of(codes, level, leaves, p):
    wide = codes.shape[2]
    lanes = lax.broadcasted_iota(jnp.int32, (8, 4 * LANES), 1) // LANES
    offset = jnp.where(lanes < 2, lanes - 3, lanes)
    cluster = lax.broadcasted_iota(jnp.int32, (8, 4 * LANES), 0)
    diagonal = lax.broadcasted_iota(jnp.int32, (8, wide), 0) == lax.broadcasted_iota(jnp.int32, (8, wide), 1)
    count = leaves >> level
    index = p * count if count > 0 else p >> level - (leaves.bit_length() - 1)
    hit = jnp.zeros(lanes.shape, jnp.bool_)
    for slot in range(codes.shape[1]):
        row = jnp.broadcast_to(codes[level, slot : slot + 1], (8, wide))
        row = pltpu.roll(row, lax.rem(wide - index, wide), 1)
        code = jnp.sum(jnp.where(diagonal, row, 0).astype(F32), axis=1, keepdims=True)
        hit = hit | (lanes.astype(F32) == code)
    partner = index + cluster + offset
    hit = hit & (partner >= 0) & (partner < wide >> level)
    return jnp.where(hit, 1.0, 0.0)


def lowered(value, table, size):
    rank = value.shape[1]
    out = mm2(value, table, mm_t)
    parts = [out[i : i + size, j : j + rank] for i in range(0, out.shape[0], size) for j in (0, rank)]
    return stack(*parts)


def spread_tables(transfer, couple, spread):
    rank = transfer.shape[-1]
    leaves = spread.shape[1] // rank
    table = lambda level: transfer[level].reshape(2 * rank, rank)
    beside = lambda rows: side(*[rows[i : i + rank] for i in range(0, rows.shape[0], rank)])
    both = stack(transfer[2, 0].astype(F32).T, transfer[2, 1].astype(F32).T, couple[2, 0].astype(F32), couple[2, 3].astype(F32))
    both = beside(lowered(lowered(both, table(1), rank), table(0), rank))
    wide = leaves * rank
    high = both[:, :wide].astype(BF)
    spread[:rank] = high
    spread[rank : 2 * rank] = high
    spread[2 * rank : 3 * rank] = (both[:, :wide] - high.astype(F32)).astype(BF)
    first, second = both[:, wide : wide * 3 // 2].astype(BF), both[:, wide * 3 // 2 :].astype(BF)
    none = jnp.zeros_like(first)
    spread[3 * rank : 4 * rank] = side(first, none)
    spread[4 * rank :] = side(none, second)


def plan_kernel(facing, away, own0, own1, codes, transfer, couple, state, spread, links_out, masks, *lifts):
    rank = transfer.shape[-1]
    levels = masks.shape[0] // 8 - 3
    leaves = spread.shape[1] // rank
    p = lax.axis_index(AXES)
    table = lambda level: transfer[level].reshape(2 * rank, rank)

    mask = [mask_of(codes, level, leaves, p) for level in range(3 + levels)]
    masks[...] = stack(*mask)
    state[...] = couplings(facing, away, own0, own1, mask, transfer, couple)
    spread_tables(transfer, couple, spread)

    for k in range(levels):
        value = couple[3 + k].reshape(4 * rank, rank).astype(F32)
        for i in reversed(range(k)):
            value = mm2(value, transfer[3 + i, (p >> i) & 1], mm_t)
        links_out[4 * rank * k : 4 * rank * (k + 1)] = halves(value, 1)

    value = table(2).astype(F32) * ROOT_HALF
    for k, lift in enumerate(lifts):
        if k > 0:
            b = (p >> (k - 1)) & 1
            value = stack(*[mm2(value, transfer[2 + k, bit]) * ROOT_HALF for bit in (b, 1 - b)])
        lift[...] = halves(value, 1)


def sides_of(facing, away):
    p = lax.axis_index(AXES)
    even = p % 2 == 0
    away = jnp.where((p > 0) & (p < lax.axis_size(AXES) - 1), away, jnp.zeros_like(away))
    return jnp.where(even, away, facing), jnp.where(even, facing, away)


def near_kernel(first, facing, away, x, blocks, near):
    _, _, size, _ = blocks.shape
    leaves = x.shape[1] // size
    rows = x.shape[0]
    left, right = sides_of(facing[: 2 * rows], away[: 2 * rows])
    before = side(left[:rows], left[rows:])
    after = side(right[:rows], right[rows:])
    at = lambda i: before if i < 0 else after if i == leaves else x[:, i * size : (i + 1) * size]
    for i in range(first, first + near.shape[1] // size):
        total = mm_t(at(i), blocks[i, 1])
        total += mm_t(at(i - 1), blocks[i, 0])
        total += mm_t(at(i + 1), blocks[i, 2])
        near[:, (i - first) * size : (i - first + 1) * size] = total


def couplings(facing, away, own0, own1, mask, transfer, couple):
    rank = transfer.shape[-1]
    leaves = mask[0].shape[0]
    rows = own0.shape[0] // leaves * 2
    table = lambda level: transfer[level].reshape(2 * rank, rank)
    left, right = sides_of(facing[...], away[...])
    block = lambda a, i: a[i * rows : (i + 1) * rows]
    lo = slice(0, rank)
    hi = slice(rank, 2 * rank)

    def coupled(level, ext, count):
        weights = mask[level].astype(BF)
        lhs = [side(*[ext[c + 3 + o] for o in OFFSETS]) * weights[c : c + 1] for c in range(count)]
        return mm(stack(*lhs), couple[level].reshape(4 * rank, rank))

    zero = jnp.zeros((rows, rank), BF)
    ext = [zero, block(left, 5)[:, lo], block(left, 5)[:, hi], zero, zero]
    ext += [block(right, 5)[:, lo], block(right, 5)[:, hi], zero]
    far2 = coupled(2, ext, 2)
    ext = [block(left, 4)[:, hi], block(left, 3)[:, lo], block(left, 3)[:, hi]]
    ext += [block(own1, c // 2)[:, (lo, hi)[c % 2]] for c in range(leaves // 2)]
    ext += [block(right, 3)[:, lo], block(right, 3)[:, hi], block(right, 4)[:, hi]]
    far1 = coupled(1, ext, leaves // 2)
    ext = [block(left, 4)[:, lo], block(left, 2)[:, lo], block(left, 2)[:, hi]]
    ext += [block(own0, c // 2)[:, (lo, hi)[c % 2]] for c in range(leaves)]
    ext += [block(right, 2)[:, lo], block(right, 2)[:, hi], block(right, 4)[:, lo]]
    far0 = coupled(0, ext, leaves)
    down = far0 + lowered(far1 + lowered(far2, table(1), rows), table(0), rows)
    return side(*[block(down, c) for c in range(leaves)])


def dense_plan_kernel(
    levels, slots, facing, away, own0, own1, codes, transfer, couple, state, spread, masks, weights, chosen
):
    rank = transfer.shape[-1]
    leaves = spread.shape[1] // rank
    p = lax.axis_index(AXES)

    mask = [mask_of(codes, level, leaves, p) for level in range(3)]
    masks[:8] = mask[2]
    masks[8:] = mask_of(codes, 2, leaves, p ^ 1)
    state[...] = couplings(facing, away, own0, own1, mask, transfer, couple)
    spread_tables(transfer, couple, spread)

    for k in range(levels):
        value = couple[3 + k].reshape(4 * rank, rank).astype(F32)
        for i in reversed(range(1, k)):
            value = mm2(value, transfer[3 + i, (p >> i) & 1], mm_t)
        for j in range(2):
            device = p ^ j
            low = mm2(value, transfer[3, device & 1], mm_t) if k > 0 else value
            hit = mask_of(codes, 3 + k, leaves, device)
            for q in range(4):
                part = low[q * rank : (q + 1) * rank] * hit[:1, q * rank : (q + 1) * rank]
                chosen[2 * k + j, q] = part.astype(BF)
            chosen[2 * k + j, 4] = jnp.zeros((rank, rank), BF)

    lifts = [[transfer[2].reshape(2 * rank, rank).astype(F32) * ROOT_HALF]]
    for k in range(1, levels):
        b = (p >> (k - 1)) & 1
        lifts.append([mm2(a, transfer[2 + k, bit]) * ROOT_HALF for bit in (b, 1 - b) for a in lifts[-1]])
    lifts = [[halves(a, 0) for a in level] for level in lifts]

    for i, slot in enumerate(slots):
        picked = []
        for k in range(levels):
            both = []
            for j in range(2):
                apart = ((p ^ slot) >> k) - ((p ^ j) >> k)
                q = jnp.where(apart < 0, apart + 3, apart)
                q = jnp.where((apart >= -3) & (apart <= 3) & (apart * apart >= 4), q, 4)
                both.append(chosen[2 * k + j, q])
            picked.append(side(*both))
        lift = side(*[lifts[k][slot & ((1 << k) - 1)] for k in range(levels)])
        out = mm(lift, stack(*picked))
        weights[2 * rank * i : 2 * rank * (i + 1)] = halves(out[: 2 * rank] + out[2 * rank :], 1)


def half_kernel(devices, slots, waits, masks, weights, *refs):
    *parts, mine, theirs, gathered = refs
    parts = parts[: len(parts) - waits]
    rank = weights.shape[1] // 4
    rows = mine.shape[0]
    p = lax.axis_index(AXES)
    gathered[...] = jnp.zeros(gathered.shape, BF)
    found = [part[i : i + rows] for part in parts for i in range(0, part.shape[0], rows)]
    for slot, value in zip(slots, found):
        gathered[slot] = value
    top = mm(side(*found), weights[...])
    top = top[:, : 2 * rank] + top[:, 2 * rank :]
    for j, out in ((0, mine), (1, theirs)):
        device = p ^ j
        at = lambda o: gathered[p ^ jnp.clip(device + o, 0, devices - 1)]
        hit = masks[8 * j : 8 * j + 8].astype(BF)
        before = at(-2)[:, rank:] * hit[0:1, :rank]
        after = at(2)[:, :rank] * hit[1:2, 3 * rank :]
        out[...] = side(halves(top[:, j * rank : (j + 1) * rank], 1), before, after)


def leaves_kernel(count, mine, theirs, state, spread, bases, *refs):
    out = refs[-1]
    leaves, rank, size = bases.shape
    near = [(ref, i) for ref in refs[:count] for i in range(0, ref.shape[1], size)]
    a, b = mine[...].astype(F32), theirs[...].astype(F32)
    top = (a[:, :rank] + b[:, :rank]) + (a[:, rank : 2 * rank] + b[:, rank : 2 * rank])
    lhs = side(halves(top, 1), top.astype(BF), (a[:, 2 * rank :] + b[:, 2 * rank :]).astype(BF))
    coef = (mm(lhs, spread[...]) + state[...]).astype(BF)
    for c in range(leaves):
        ref, at = near[c]
        total = mm(coef[:, c * rank : (c + 1) * rank], bases[c]) + ref[:, at : at + size]
        out[:, c * size : (c + 1) * size] = total.astype(BF)


def climb(up, count, transfer, level, bit, rows):
    rank = up.shape[1]
    pairs = up.reshape(count // 2, 2, rows, rank)
    children = [pairs[:, i].reshape(count // 2 * rows, rank) for i in range(2)]
    turned = stack(transfer[level, bit], transfer[level, 1 - bit])
    return mm2(side(*children), turned) * ROOT_HALF


def down_kernel(devices, stages, levels, *refs):
    refs = list(refs)
    slots = slots_of(stages)
    received = refs[: len(slots)]
    refs = refs[len(slots) :]
    lifts = [refs.pop(0) for _ in range(min(levels, 3))]
    state, spread, links, masks, transfer, bases, near, out, gathered, *ups = refs
    leaves, rank, size = bases.shape
    rows = out.shape[0]
    p = lax.axis_index(AXES)

    for part, ref in zip(slots, received):
        for i, slot in enumerate(part):
            gathered[slot] = ref[i * rows : (i + 1) * rows]

    def raised(k, first, count):
        sets = [side(*[gathered[first[i] + j] for j in range(1 << k)]) for i in range(count)]
        up = mm(stack(*sets), lifts[k][...])
        return up[:, :rank] + up[:, rank:]

    if ups:
        count = devices >> 2
        up = raised(2, [4 * i for i in range(count)], count)
        for k in range(3, levels):
            up = climb(up, count, transfer, 2 + k, (p >> (k - 1)) & 1, rows)
            count //= 2
            ups[k - 3][...] = up.reshape(count, rows, rank)
    lhs = []
    for k in range(levels):
        a = p >> k
        n = devices >> k
        places = [a ^ jnp.clip(a + o, 0, n - 1) for o in OFFSETS]
        if k < 3:
            up = raised(k, [place << k for place in places], 4)
            parts = [up[i * rows : (i + 1) * rows] for i in range(4)]
        else:
            parts = [ups[k - 3][place] for place in places]
        lhs.append(side(*parts) * masks[8 * (3 + k) : 8 * (3 + k) + 1])
    top = mm(halves(side(*lhs), 0), links[...])
    top = top[:rows, :rank] + top[:rows, rank:] + top[rows:, :rank] + top[rows:, rank:]

    at = lambda o: gathered[p ^ jnp.clip(p + o, 0, devices - 1)]
    weights = masks[16:24].astype(BF)
    before = at(-2)[:, rank:] * weights[0:1, :rank]
    after = at(2)[:, :rank] * weights[1:2, 3 * rank :]
    lhs = side(halves(top, 1), top.astype(BF), before, after)
    coef = (mm(lhs, spread[...]) + state[...]).astype(BF)
    for c in range(leaves):
        cols = slice(c * size, (c + 1) * size)
        out[:, cols] = (mm(coef[:, c * rank : (c + 1) * rank], bases[c]) + near[:, cols]).astype(BF)


def inside(x):
    return pltpu.with_memory_space_constraint(x, pltpu.VMEM)


def outside(x):
    return pltpu.with_memory_space_constraint(x, pltpu.HBM)


def shards(rhs, bases, near_blocks, transfer, couple, codes):
    rows = rhs.shape[0]
    leaves, rank, size = bases.shape
    devices = lax.axis_size(AXES)
    stages = stages_of(devices)
    levels = devices.bit_length() - 2
    params = pltpu.CompilerParams(vmem_limit_bytes=16 << 20)

    def call(kernel, shapes, operands, name, flops=0, place=inside, **more):
        single = not isinstance(shapes, list)
        return pl.pallas_call(
            kernel,
            out_shape=shapes if single else list(shapes),
            compiler_params=params,
            cost_estimate=pl.CostEstimate(flops=flops, bytes_accessed=1 << 20, transcendentals=0),
            name=name,
            **more,
        )(*map(place, operands))

    x, bases, facing, away, own0, own1, own2 = call(
        first_kernel,
        [
            pltpu.VMEM(rhs.shape, BF),
            pltpu.VMEM(bases.shape, BF),
            pltpu.VMEM((6 * rows, 2 * rank), BF),
            pltpu.VMEM((6 * rows, 2 * rank), BF),
            pltpu.VMEM((leaves // 2 * rows, 2 * rank), BF),
            pltpu.VMEM((leaves // 4 * rows, 2 * rank), BF),
            pltpu.VMEM((rows, 2 * rank), BF),
        ],
        (rhs, bases, transfer),
        "first",
        1 << 32,
        place=outside,
        in_specs=[pl.BlockSpec(memory_space=pl.ANY)] * 3,
        scratch_shapes=[pltpu.VMEM((2, 2, rank, rank), BF), pltpu.SemaphoreType.DMA((3,))],
    )

    facing = exchanged(facing, 1)
    away = across_pairs(away)

    dense = levels <= 3
    if dense:
        slots = [slot for part in slots_of(stages)[:-1] for slot in part]
        state, spread, masks, weights = call(
            functools.partial(dense_plan_kernel, levels, slots),
            [
                pltpu.VMEM((rows, leaves * rank), F32),
                pltpu.VMEM((5 * rank, leaves * rank), BF),
                pltpu.VMEM((16, 4 * rank), F32),
                pltpu.VMEM((2 * rank * len(slots), 4 * rank), BF),
            ],
            (facing, away, own0, own1, codes, transfer, couple),
            "plan",
            1 << 30,
            scratch_shapes=[pltpu.VMEM((2 * levels, 5, rank, rank), BF)],
        )
    else:
        lifts = [pltpu.VMEM(((2 << k) * rank, 2 * rank), BF) for k in range(min(levels, 3))]
        state, spread, links, masks, *lifts = call(
            plan_kernel,
            [
                pltpu.VMEM((rows, leaves * rank), F32),
                pltpu.VMEM((5 * rank, leaves * rank), BF),
                pltpu.VMEM((levels * 4 * rank, 2 * rank), BF),
                pltpu.VMEM((8 * (3 + levels), 4 * rank), F32),
                *lifts,
            ],
            (facing, away, own0, own1, codes, transfer, couple),
            "plan",
            1 << 30,
        )

    def near_of(first, count):
        return call(
            functools.partial(near_kernel, first),
            pltpu.VMEM((rows, count * size), F32),
            (facing, away, x, near_blocks),
            "near_field",
            3 * count * rows * size * size * 2,
        )

    some = leaves * SHARE // 8 if dense else 0
    near = (near_of(0, some),) if some else ()
    gathered = own2
    received = [own2]
    for group in stages[:-1]:
        got = [exchanged(gathered, m) for m in group]
        received += got
        if group is not stages[-2]:
            gathered = stack(gathered, *got)
    if dense:
        mine, theirs = call(
            functools.partial(half_kernel, devices, slots, len(near)),
            [pltpu.VMEM((rows, 4 * rank), BF), pltpu.VMEM((rows, 4 * rank), BF)],
            (masks, weights, *received, *near),
            "half",
            scratch_shapes=[pltpu.VMEM((devices, rows, 2 * rank), BF)],
        )
        theirs = exchanged(theirs, 1)
    else:
        parts = (gathered, *got) if len(stages) > 1 else (gathered,)
        pay = call(
            pack_kernel,
            pltpu.VMEM((sum(part.shape[0] for part in parts), 2 * rank), BF),
            (masks, *parts),
            "pack",
        )
        received.append(exchanged(pay, 1))

    near = (*near, near_of(some, leaves - some))
    if dense:
        return call(
            functools.partial(leaves_kernel, len(near)),
            jax.ShapeDtypeStruct((rows, leaves * size), BF),
            (mine, theirs, state, spread, bases, *near, *received, masks, weights, transfer),
            "leaves",
        )
    return call(
        functools.partial(down_kernel, devices, stages, levels),
        jax.ShapeDtypeStruct((rows, leaves * size), BF),
        (*received, *lifts, state, spread, links, masks, transfer, bases, *near),
        "down_sweep",
        scratch_shapes=[pltpu.VMEM((devices, rows, 2 * rank), BF)]
        + [pltpu.VMEM((devices >> k, rows, rank), F32) for k in range(3, levels)],
    )


def solution(mesh):
    return jax.shard_map(
        shards,
        mesh=mesh,
        in_specs=(
            P(None, ("groups", "leaf", "sub")),
            P(("groups", "leaf", "sub"), None, None),
            P(("groups", "leaf", "sub"), None, None, None),
            P(),
            P(),
            P(),
        ),
        out_specs=P(None, ("groups", "leaf", "sub")),
        check_vma=False,
    )
```

```python
import functools

import jax
import jax.numpy as jnp
from jax import lax
from jax.experimental import pallas as pl
from jax.experimental.pallas import tpu as pltpu
from jax.sharding import PartitionSpec as P

ROOT_HALF = 0.7071067811865476
OFFSETS = (-3, -2, 2, 3)
AXES = ("leaf", "sub")
BF = jnp.bfloat16
F32 = jnp.float32
LANES = 64
SHARE = 2


def mm(a, b):
    return lax.dot_general(a, b, (((1,), (0,)), ((), ())), preferred_element_type=F32)


def mm_t(a, b):
    return lax.dot_general(a, b, (((1,), (1,)), ((), ())), preferred_element_type=F32)


def split(a):
    high = a.astype(BF)
    low = (a - high.astype(F32)).astype(BF)
    return jnp.concatenate([high, low], axis=0)


def mm2(a, b, product=mm):
    out = product(split(a), b)
    return out[: a.shape[0]] + out[a.shape[0] :]


def halves(a, axis):
    high = a.astype(BF)
    return jnp.concatenate([high, (a - high.astype(F32)).astype(BF)], axis=axis)


def side(*parts):
    return jnp.concatenate(parts, axis=1)


def stack(*parts):
    return jnp.concatenate(parts, axis=0)


def stages_of(devices):
    bits = [1 << b for b in range(1, devices.bit_length() - 1)]
    rounds = [(bits.pop() | 1,)] if len(bits) % 2 else []
    while bits:
        high, low = bits.pop(), bits.pop()
        rounds.append((low | 1, high | 1, low | high))
    return rounds + [(1,)]


def slots_of(stages):
    held = [[0]]
    for masks in stages:
        so_far = [slot for part in held for slot in part]
        held += [[slot ^ m for slot in so_far] for m in masks]
    return held


def exchanged(x, apart):
    devices = lax.axis_size(AXES)
    return lax.ppermute(x, AXES, [(i, i ^ apart) for i in range(devices)])


def across_pairs(x):
    groups, devices = lax.axis_size("groups"), lax.axis_size(AXES)
    pairs = []
    for g in range(groups):
        for i in range(devices):
            j = i + 1 if i % 2 else i - 1
            to = (g, j) if 0 <= j < devices else ((g + 1) % groups, i)
            pairs.append((g * devices + i, to[0] * devices + to[1]))
    return lax.ppermute(x, ("groups", *AXES), pairs)


def first_kernel(rhs_hbm, bases_hbm, transfer_hbm, x, bases, facing, away, own0, own1, own2, low, sems):
    leaves, rank, size = bases.shape
    rows = x.shape[0]
    pairs = (
        (transfer_hbm.at[pl.ds(0, 2)], low),
        (bases_hbm, bases),
        (rhs_hbm, x),
    )
    copies = [pltpu.make_async_copy(*pair, sems.at[i]) for i, pair in enumerate(pairs)]
    for copy in copies:
        copy.start()
    copies[0].wait()
    table = low[0].reshape(2 * rank, rank)
    product = halves(stack(mm(table, low[1, 0]), mm(table, low[1, 1])) * (ROOT_HALF * ROOT_HALF), 1)
    copies[1].wait()
    copies[2].wait()
    at = lambda i: x[:, i * size : (i + 1) * size]
    first = lax.broadcasted_iota(jnp.int32, (rows, 2 * rank), 1) < rank
    parts = []
    for i in range(0, leaves, 2):
        both = mm_t(stack(at(i), at(i + 1)), bases[i : i + 2].reshape(2 * rank, size))
        parts.append(jnp.where(first, both[:rows], both[rows:]))
    leaf_coef = stack(*parts)
    fours = stack(*[side(parts[i], parts[i + 1]) for i in range(0, leaves // 2, 2)])
    up = mm(halves(fours, 0), product)
    count = fours.shape[0]
    up = up[:count, :rank] + up[:count, rank:] + up[count:, :rank]
    own2[...] = side(*[up[i : i + rows] for i in range(0, count, rows)]).astype(BF)
    u2 = own2

    own0[...] = leaf_coef.astype(BF)
    up1 = mm2(leaf_coef, table) * ROOT_HALF
    up1 = [up1[i : i + rows] for i in range(0, up1.shape[0], rows)]
    own1[...] = stack(*[side(up1[i], up1[i + 1]) for i in range(0, len(up1), 2)]).astype(BF)
    end = x.shape[1]
    half = size // 2
    last0, last1 = own0.shape[0] - rows, own1.shape[0] - rows
    right = stack(
        x[:, end - size : end - half],
        x[:, end - half :],
        own0[last0:],
        own1[last1:],
        side(own0[last0 - rows : last0, rank:], own1[last1 - rows : last1, rank:]),
        u2[...],
    )
    left = stack(
        x[:, :half],
        x[:, half:size],
        own0[:rows],
        own1[:rows],
        side(own0[rows : 2 * rows, :rank], own1[rows : 2 * rows, :rank]),
        u2[...],
    )
    even = lax.axis_index(AXES) % 2 == 0
    facing[...] = jnp.where(even, right, left)
    away[...] = jnp.where(even, left, right)


def pack_kernel(after, *refs):
    *parts, out = refs
    at = 0
    for part in parts:
        out[at : at + part.shape[0]] = part[...]
        at += part.shape[0]


def mask_of(codes, level, leaves, p):
    wide = codes.shape[2]
    lanes = lax.broadcasted_iota(jnp.int32, (8, 4 * LANES), 1) // LANES
    offset = jnp.where(lanes < 2, lanes - 3, lanes)
    cluster = lax.broadcasted_iota(jnp.int32, (8, 4 * LANES), 0)
    diagonal = lax.broadcasted_iota(jnp.int32, (8, wide), 0) == lax.broadcasted_iota(jnp.int32, (8, wide), 1)
    count = leaves >> level
    index = p * count if count > 0 else p >> level - (leaves.bit_length() - 1)
    hit = jnp.zeros(lanes.shape, jnp.bool_)
    for slot in range(codes.shape[1]):
        row = jnp.broadcast_to(codes[level, slot : slot + 1], (8, wide))
        row = pltpu.roll(row, lax.rem(wide - index, wide), 1)
        code = jnp.sum(jnp.where(diagonal, row, 0).astype(F32), axis=1, keepdims=True)
        hit = hit | (lanes.astype(F32) == code)
    partner = index + cluster + offset
    hit = hit & (partner >= 0) & (partner < wide >> level)
    return jnp.where(hit, 1.0, 0.0)


def lowered(value, table, size):
    rank = value.shape[1]
    out = mm2(value, table, mm_t)
    parts = [out[i : i + size, j : j + rank] for i in range(0, out.shape[0], size) for j in (0, rank)]
    return stack(*parts)


def spread_tables(transfer, couple, spread):
    rank = transfer.shape[-1]
    leaves = spread.shape[1] // rank
    table = lambda level: transfer[level].reshape(2 * rank, rank)
    beside = lambda rows: side(*[rows[i : i + rank] for i in range(0, rows.shape[0], rank)])
    both = stack(transfer[2, 0].astype(F32).T, transfer[2, 1].astype(F32).T, couple[2, 0].astype(F32), couple[2, 3].astype(F32))
    both = beside(lowered(lowered(both, table(1), rank), table(0), rank))
    wide = leaves * rank
    high = both[:, :wide].astype(BF)
    spread[:rank] = high
    spread[rank : 2 * rank] = high
    spread[2 * rank : 3 * rank] = (both[:, :wide] - high.astype(F32)).astype(BF)
    first, second = both[:, wide : wide * 3 // 2].astype(BF), both[:, wide * 3 // 2 :].astype(BF)
    none = jnp.zeros_like(first)
    spread[3 * rank : 4 * rank] = side(first, none)
    spread[4 * rank :] = side(none, second)


def plan_kernel(facing, away, own0, own1, codes, transfer, couple, state, spread, links_out, masks, *lifts):
    rank = transfer.shape[-1]
    levels = masks.shape[0] // 8 - 3
    leaves = spread.shape[1] // rank
    p = lax.axis_index(AXES)
    table = lambda level: transfer[level].reshape(2 * rank, rank)

    mask = [mask_of(codes, level, leaves, p) for level in range(3 + levels)]
    masks[...] = stack(*mask)
    state[...] = couplings(facing, away, own0, own1, mask, transfer, couple)
    spread_tables(transfer, couple, spread)

    for k in range(levels):
        value = couple[3 + k].reshape(4 * rank, rank).astype(F32)
        for i in reversed(range(k)):
            value = mm2(value, transfer[3 + i, (p >> i) & 1], mm_t)
        links_out[4 * rank * k : 4 * rank * (k + 1)] = halves(value, 1)

    value = table(2).astype(F32) * ROOT_HALF
    for k, lift in enumerate(lifts):
        if k > 0:
            b = (p >> (k - 1)) & 1
            value = stack(*[mm2(value, transfer[2 + k, bit]) * ROOT_HALF for bit in (b, 1 - b)])
        lift[...] = halves(value, 1)


def sides_of(facing, away):
    p = lax.axis_index(AXES)
    even = p % 2 == 0
    away = jnp.where((p > 0) & (p < lax.axis_size(AXES) - 1), away, jnp.zeros_like(away))
    return jnp.where(even, away, facing), jnp.where(even, facing, away)


def near_kernel(first, facing, away, x, blocks, near):
    _, _, size, _ = blocks.shape
    leaves = x.shape[1] // size
    rows = x.shape[0]
    left, right = sides_of(facing[: 2 * rows], away[: 2 * rows])
    before = side(left[:rows], left[rows:])
    after = side(right[:rows], right[rows:])
    at = lambda i: before if i < 0 else after if i == leaves else x[:, i * size : (i + 1) * size]
    for i in range(first, first + near.shape[1] // size):
        total = mm_t(at(i), blocks[i, 1])
        total += mm_t(at(i - 1), blocks[i, 0])
        total += mm_t(at(i + 1), blocks[i, 2])
        near[:, (i - first) * size : (i - first + 1) * size] = total


def couplings(facing, away, own0, own1, mask, transfer, couple):
    rank = transfer.shape[-1]
    leaves = mask[0].shape[0]
    rows = own0.shape[0] // leaves * 2
    table = lambda level: transfer[level].reshape(2 * rank, rank)
    left, right = sides_of(facing[...], away[...])
    block = lambda a, i: a[i * rows : (i + 1) * rows]
    lo = slice(0, rank)
    hi = slice(rank, 2 * rank)

    def coupled(level, ext, count):
        weights = mask[level].astype(BF)
        lhs = [side(*[ext[c + 3 + o] for o in OFFSETS]) * weights[c : c + 1] for c in range(count)]
        return mm(stack(*lhs), couple[level].reshape(4 * rank, rank))

    zero = jnp.zeros((rows, rank), BF)
    ext = [zero, block(left, 5)[:, lo], block(left, 5)[:, hi], zero, zero]
    ext += [block(right, 5)[:, lo], block(right, 5)[:, hi], zero]
    far2 = coupled(2, ext, 2)
    ext = [block(left, 4)[:, hi], block(left, 3)[:, lo], block(left, 3)[:, hi]]
    ext += [block(own1, c // 2)[:, (lo, hi)[c % 2]] for c in range(leaves // 2)]
    ext += [block(right, 3)[:, lo], block(right, 3)[:, hi], block(right, 4)[:, hi]]
    far1 = coupled(1, ext, leaves // 2)
    ext = [block(left, 4)[:, lo], block(left, 2)[:, lo], block(left, 2)[:, hi]]
    ext += [block(own0, c // 2)[:, (lo, hi)[c % 2]] for c in range(leaves)]
    ext += [block(right, 2)[:, lo], block(right, 2)[:, hi], block(right, 4)[:, lo]]
    far0 = coupled(0, ext, leaves)
    down = far0 + lowered(far1 + lowered(far2, table(1), rows), table(0), rows)
    return side(*[block(down, c) for c in range(leaves)])


def dense_plan_kernel(
    levels, slots, away, facing, own0, own1, codes, transfer, couple, state, spread, masks, weights, chosen
):
    rank = transfer.shape[-1]
    leaves = spread.shape[1] // rank
    p = lax.axis_index(AXES)

    mask = [mask_of(codes, level, leaves, p) for level in range(3)]
    masks[:8] = mask[2]
    masks[8:] = mask_of(codes, 2, leaves, p ^ 1)
    state[...] = couplings(facing, away, own0, own1, mask, transfer, couple)
    spread_tables(transfer, couple, spread)

    for k in range(levels):
        value = couple[3 + k].reshape(4 * rank, rank).astype(F32)
        for i in reversed(range(1, k)):
            value = mm2(value, transfer[3 + i, (p >> i) & 1], mm_t)
        for j in range(2):
            device = p ^ j
            low = mm2(value, transfer[3, device & 1], mm_t) if k > 0 else value
            hit = mask_of(codes, 3 + k, leaves, device)
            for q in range(4):
                part = low[q * rank : (q + 1) * rank] * hit[:1, q * rank : (q + 1) * rank]
                chosen[2 * k + j, q] = part.astype(BF)
            chosen[2 * k + j, 4] = jnp.zeros((rank, rank), BF)

    lifts = [[transfer[2].reshape(2 * rank, rank).astype(F32) * ROOT_HALF]]
    for k in range(1, levels):
        b = (p >> (k - 1)) & 1
        lifts.append([mm2(a, transfer[2 + k, bit]) * ROOT_HALF for bit in (b, 1 - b) for a in lifts[-1]])
    lifts = [[halves(a, 0) for a in level] for level in lifts]

    for i, slot in enumerate(slots):
        picked = []
        for k in range(levels):
            both = []
            for j in range(2):
                apart = ((p ^ slot) >> k) - ((p ^ j) >> k)
                q = jnp.where(apart < 0, apart + 3, apart)
                q = jnp.where((apart >= -3) & (apart <= 3) & (apart * apart >= 4), q, 4)
                both.append(chosen[2 * k + j, q])
            picked.append(side(*both))
        lift = side(*[lifts[k][slot & ((1 << k) - 1)] for k in range(levels)])
        out = mm(lift, stack(*picked))
        weights[2 * rank * i : 2 * rank * (i + 1)] = halves(out[: 2 * rank] + out[2 * rank :], 1)


def half_kernel(devices, slots, waits, masks, weights, *refs):
    *parts, mine, theirs, gathered = refs
    parts = parts[: len(parts) - waits]
    rank = weights.shape[1] // 4
    rows = mine.shape[0]
    p = lax.axis_index(AXES)
    gathered[...] = jnp.zeros(gathered.shape, BF)
    found = [part[i : i + rows] for part in parts for i in range(0, part.shape[0], rows)]
    for slot, value in zip(slots, found):
        gathered[slot] = value
    top = mm(side(*found), weights[...])
    top = top[:, : 2 * rank] + top[:, 2 * rank :]
    for j, out in ((0, mine), (1, theirs)):
        device = p ^ j
        at = lambda o: gathered[p ^ jnp.clip(device + o, 0, devices - 1)]
        hit = masks[8 * j : 8 * j + 8].astype(BF)
        before = at(-2)[:, rank:] * hit[0:1, :rank]
        after = at(2)[:, :rank] * hit[1:2, 3 * rank :]
        out[...] = side(halves(top[:, j * rank : (j + 1) * rank], 1), before, after)


def leaves_kernel(count, mine, theirs, state, spread, bases, *refs):
    out = refs[-1]
    leaves, rank, size = bases.shape
    near = [(ref, i) for ref in refs[:count] for i in range(0, ref.shape[1], size)]
    a, b = mine[...].astype(F32), theirs[...].astype(F32)
    top = (a[:, :rank] + b[:, :rank]) + (a[:, rank : 2 * rank] + b[:, rank : 2 * rank])
    lhs = side(halves(top, 1), top.astype(BF), (a[:, 2 * rank :] + b[:, 2 * rank :]).astype(BF))
    coef = (mm(lhs, spread[...]) + state[...]).astype(BF)
    for c in range(leaves):
        ref, at = near[c]
        total = mm(coef[:, c * rank : (c + 1) * rank], bases[c]) + ref[:, at : at + size]
        out[:, c * size : (c + 1) * size] = total.astype(BF)


def climb(up, count, transfer, level, bit, rows):
    rank = up.shape[1]
    pairs = up.reshape(count // 2, 2, rows, rank)
    children = [pairs[:, i].reshape(count // 2 * rows, rank) for i in range(2)]
    turned = stack(transfer[level, bit], transfer[level, 1 - bit])
    return mm2(side(*children), turned) * ROOT_HALF


def down_kernel(devices, stages, levels, *refs):
    refs = list(refs)
    slots = slots_of(stages)
    received = refs[: len(slots)]
    refs = refs[len(slots) :]
    lifts = [refs.pop(0) for _ in range(min(levels, 3))]
    state, spread, links, masks, transfer, bases, near, out, gathered, *ups = refs
    leaves, rank, size = bases.shape
    rows = out.shape[0]
    p = lax.axis_index(AXES)

    for part, ref in zip(slots, received):
        for i, slot in enumerate(part):
            gathered[slot] = ref[i * rows : (i + 1) * rows]

    def raised(k, first, count):
        sets = [side(*[gathered[first[i] + j] for j in range(1 << k)]) for i in range(count)]
        up = mm(stack(*sets), lifts[k][...])
        return up[:, :rank] + up[:, rank:]

    if ups:
        count = devices >> 2
        up = raised(2, [4 * i for i in range(count)], count)
        for k in range(3, levels):
            up = climb(up, count, transfer, 2 + k, (p >> (k - 1)) & 1, rows)
            count //= 2
            ups[k - 3][...] = up.reshape(count, rows, rank)
    lhs = []
    for k in range(levels):
        a = p >> k
        n = devices >> k
        places = [a ^ jnp.clip(a + o, 0, n - 1) for o in OFFSETS]
        if k < 3:
            up = raised(k, [place << k for place in places], 4)
            parts = [up[i * rows : (i + 1) * rows] for i in range(4)]
        else:
            parts = [ups[k - 3][place] for place in places]
        lhs.append(side(*parts) * masks[8 * (3 + k) : 8 * (3 + k) + 1])
    top = mm(halves(side(*lhs), 0), links[...])
    top = top[:rows, :rank] + top[:rows, rank:] + top[rows:, :rank] + top[rows:, rank:]

    at = lambda o: gathered[p ^ jnp.clip(p + o, 0, devices - 1)]
    weights = masks[16:24].astype(BF)
    before = at(-2)[:, rank:] * weights[0:1, :rank]
    after = at(2)[:, :rank] * weights[1:2, 3 * rank :]
    lhs = side(halves(top, 1), top.astype(BF), before, after)
    coef = (mm(lhs, spread[...]) + state[...]).astype(BF)
    for c in range(leaves):
        cols = slice(c * size, (c + 1) * size)
        out[:, cols] = (mm(coef[:, c * rank : (c + 1) * rank], bases[c]) + near[:, cols]).astype(BF)


def inside(x):
    return pltpu.with_memory_space_constraint(x, pltpu.VMEM)


def outside(x):
    return pltpu.with_memory_space_constraint(x, pltpu.HBM)


def shards(rhs, bases, near_blocks, transfer, couple, codes):
    rows = rhs.shape[0]
    leaves, rank, size = bases.shape
    devices = lax.axis_size(AXES)
    stages = stages_of(devices)
    levels = devices.bit_length() - 2
    params = pltpu.CompilerParams(vmem_limit_bytes=16 << 20)

    def call(kernel, shapes, operands, name, flops=0, place=inside, **more):
        single = not isinstance(shapes, list)
        return pl.pallas_call(
            kernel,
            out_shape=shapes if single else list(shapes),
            compiler_params=params,
            cost_estimate=pl.CostEstimate(flops=flops, bytes_accessed=1 << 20, transcendentals=0),
            name=name,
            **more,
        )(*map(place, operands))

    x, bases, facing, away, own0, own1, own2 = call(
        first_kernel,
        [
            pltpu.VMEM(rhs.shape, BF),
            pltpu.VMEM(bases.shape, BF),
            pltpu.VMEM((6 * rows, 2 * rank), BF),
            pltpu.VMEM((6 * rows, 2 * rank), BF),
            pltpu.VMEM((leaves // 2 * rows, 2 * rank), BF),
            pltpu.VMEM((leaves // 4 * rows, 2 * rank), BF),
            pltpu.VMEM((rows, 2 * rank), BF),
        ],
        (rhs, bases, transfer),
        "first",
        1 << 32,
        place=outside,
        in_specs=[pl.BlockSpec(memory_space=pl.ANY)] * 3,
        scratch_shapes=[pltpu.VMEM((2, 2, rank, rank), BF), pltpu.SemaphoreType.DMA((3,))],
    )

    facing = exchanged(facing, 1)
    away = across_pairs(away)

    dense = levels <= 3
    if dense:
        slots = [slot for part in slots_of(stages)[:-1] for slot in part]
        state, spread, masks, weights = call(
            functools.partial(dense_plan_kernel, levels, slots),
            [
                pltpu.VMEM((rows, leaves * rank), F32),
                pltpu.VMEM((5 * rank, leaves * rank), BF),
                pltpu.VMEM((16, 4 * rank), F32),
                pltpu.VMEM((2 * rank * len(slots), 4 * rank), BF),
            ],
            (away, facing, own0, own1, codes, transfer, couple),
            "plan",
            1 << 30,
            scratch_shapes=[pltpu.VMEM((2 * levels, 5, rank, rank), BF)],
        )
    else:
        lifts = [pltpu.VMEM(((2 << k) * rank, 2 * rank), BF) for k in range(min(levels, 3))]
        state, spread, links, masks, *lifts = call(
            plan_kernel,
            [
                pltpu.VMEM((rows, leaves * rank), F32),
                pltpu.VMEM((5 * rank, leaves * rank), BF),
                pltpu.VMEM((levels * 4 * rank, 2 * rank), BF),
                pltpu.VMEM((8 * (3 + levels), 4 * rank), F32),
                *lifts,
            ],
            (facing, away, own0, own1, codes, transfer, couple),
            "plan",
            1 << 30,
        )

    def near_of(first, count):
        return call(
            functools.partial(near_kernel, first),
            pltpu.VMEM((rows, count * size), F32),
            (facing, away, x, near_blocks),
            "near_field",
            3 * count * rows * size * size * 2,
        )

    some = leaves * SHARE // 8 if dense else 0
    near = (near_of(0, some),) if some else ()
    gathered = own2
    received = [own2]
    for group in stages[:-1]:
        got = [exchanged(gathered, m) for m in group]
        received += got
        if group is not stages[-2]:
            gathered = stack(gathered, *got)
    if dense:
        mine, theirs = call(
            functools.partial(half_kernel, devices, slots, len(near)),
            [pltpu.VMEM((rows, 4 * rank), BF), pltpu.VMEM((rows, 4 * rank), BF)],
            (masks, weights, *received, *near),
            "half",
            scratch_shapes=[pltpu.VMEM((devices, rows, 2 * rank), BF)],
        )
        theirs = exchanged(theirs, 1)
    else:
        parts = (gathered, *got) if len(stages) > 1 else (gathered,)
        pay = call(
            pack_kernel,
            pltpu.VMEM((sum(part.shape[0] for part in parts), 2 * rank), BF),
            (masks, *parts),
            "pack",
        )
        received.append(exchanged(pay, 1))

    near = (*near, near_of(some, leaves - some))
    if dense:
        return call(
            functools.partial(leaves_kernel, len(near)),
            jax.ShapeDtypeStruct((rows, leaves * size), BF),
            (mine, theirs, state, spread, bases, *near, *received, masks, weights, transfer),
            "leaves",
        )
    return call(
        functools.partial(down_kernel, devices, stages, levels),
        jax.ShapeDtypeStruct((rows, leaves * size), BF),
        (*received, *lifts, state, spread, links, masks, transfer, bases, *near),
        "down_sweep",
        scratch_shapes=[pltpu.VMEM((devices, rows, 2 * rank), BF)]
        + [pltpu.VMEM((devices >> k, rows, rank), F32) for k in range(3, levels)],
    )


def solution(mesh):
    return jax.shard_map(
        shards,
        mesh=mesh,
        in_specs=(
            P(None, ("groups", "leaf", "sub")),
            P(("groups", "leaf", "sub"), None, None),
            P(("groups", "leaf", "sub"), None, None, None),
            P(),
            P(),
            P(),
        ),
        out_specs=P(None, ("groups", "leaf", "sub")),
        check_vma=False,
    )
```

```python
import functools

import jax
import jax.numpy as jnp
from jax import lax
from jax.experimental import pallas as pl
from jax.experimental.pallas import tpu as pltpu
from jax.sharding import PartitionSpec as P

ROOT_HALF = 0.7071067811865476
OFFSETS = (-3, -2, 2, 3)
AXES = ("leaf", "sub")
BF = jnp.bfloat16
F32 = jnp.float32
LANES = 64
SHARE = 3


def mm(a, b):
    return lax.dot_general(a, b, (((1,), (0,)), ((), ())), preferred_element_type=F32)


def mm_t(a, b):
    return lax.dot_general(a, b, (((1,), (1,)), ((), ())), preferred_element_type=F32)


def split(a):
    high = a.astype(BF)
    low = (a - high.astype(F32)).astype(BF)
    return jnp.concatenate([high, low], axis=0)


def mm2(a, b, product=mm):
    out = product(split(a), b)
    return out[: a.shape[0]] + out[a.shape[0] :]


def halves(a, axis):
    high = a.astype(BF)
    return jnp.concatenate([high, (a - high.astype(F32)).astype(BF)], axis=axis)


def side(*parts):
    return jnp.concatenate(parts, axis=1)


def stack(*parts):
    return jnp.concatenate(parts, axis=0)


def stages_of(devices):
    bits = [1 << b for b in range(1, devices.bit_length() - 1)]
    rounds = [(bits.pop() | 1,)] if len(bits) % 2 else []
    while bits:
        high, low = bits.pop(), bits.pop()
        rounds.append((low | 1, high | 1, low | high))
    return rounds + [(1,)]


def slots_of(stages):
    held = [[0]]
    for masks in stages:
        so_far = [slot for part in held for slot in part]
        held += [[slot ^ m for slot in so_far] for m in masks]
    return held


def exchanged(x, apart):
    devices = lax.axis_size(AXES)
    return lax.ppermute(x, AXES, [(i, i ^ apart) for i in range(devices)])


def across_pairs(x):
    groups, devices = lax.axis_size("groups"), lax.axis_size(AXES)
    pairs = []
    for g in range(groups):
        for i in range(devices):
            j = i + 1 if i % 2 else i - 1
            to = (g, j) if 0 <= j < devices else ((g + 1) % groups, i)
            pairs.append((g * devices + i, to[0] * devices + to[1]))
    return lax.ppermute(x, ("groups", *AXES), pairs)


def first_kernel(rhs_hbm, bases_hbm, transfer_hbm, x, bases, facing, away, own0, own1, own2, low, sems):
    leaves, rank, size = bases.shape
    rows = x.shape[0]
    pairs = (
        (transfer_hbm.at[pl.ds(0, 2)], low),
        (bases_hbm, bases),
        (rhs_hbm, x),
    )
    copies = [pltpu.make_async_copy(*pair, sems.at[i]) for i, pair in enumerate(pairs)]
    for copy in copies:
        copy.start()
    copies[0].wait()
    table = low[0].reshape(2 * rank, rank)
    product = halves(stack(mm(table, low[1, 0]), mm(table, low[1, 1])) * (ROOT_HALF * ROOT_HALF), 1)
    copies[1].wait()
    copies[2].wait()
    at = lambda i: x[:, i * size : (i + 1) * size]
    first = lax.broadcasted_iota(jnp.int32, (rows, 2 * rank), 1) < rank
    parts = []
    for i in range(0, leaves, 2):
        both = mm_t(stack(at(i), at(i + 1)), bases[i : i + 2].reshape(2 * rank, size))
        parts.append(jnp.where(first, both[:rows], both[rows:]))
    leaf_coef = stack(*parts)
    fours = stack(*[side(parts[i], parts[i + 1]) for i in range(0, leaves // 2, 2)])
    up = mm(halves(fours, 0), product)
    count = fours.shape[0]
    up = up[:count, :rank] + up[:count, rank:] + up[count:, :rank]
    own2[...] = side(*[up[i : i + rows] for i in range(0, count, rows)]).astype(BF)
    u2 = own2

    own0[...] = leaf_coef.astype(BF)
    up1 = mm2(leaf_coef, table) * ROOT_HALF
    up1 = [up1[i : i + rows] for i in range(0, up1.shape[0], rows)]
    own1[...] = stack(*[side(up1[i], up1[i + 1]) for i in range(0, len(up1), 2)]).astype(BF)
    end = x.shape[1]
    half = size // 2
    last0, last1 = own0.shape[0] - rows, own1.shape[0] - rows
    right = stack(
        x[:, end - size : end - half],
        x[:, end - half :],
        own0[last0:],
        own1[last1:],
        side(own0[last0 - rows : last0, rank:], own1[last1 - rows : last1, rank:]),
        u2[...],
    )
    left = stack(
        x[:, :half],
        x[:, half:size],
        own0[:rows],
        own1[:rows],
        side(own0[rows : 2 * rows, :rank], own1[rows : 2 * rows, :rank]),
        u2[...],
    )
    even = lax.axis_index(AXES) % 2 == 0
    facing[...] = jnp.where(even, right, left)
    away[...] = jnp.where(even, left, right)


def pack_kernel(after, *refs):
    *parts, out = refs
    at = 0
    for part in parts:
        out[at : at + part.shape[0]] = part[...]
        at += part.shape[0]


def mask_of(codes, level, leaves, p):
    wide = codes.shape[2]
    lanes = lax.broadcasted_iota(jnp.int32, (8, 4 * LANES), 1) // LANES
    offset = jnp.where(lanes < 2, lanes - 3, lanes)
    cluster = lax.broadcasted_iota(jnp.int32, (8, 4 * LANES), 0)
    diagonal = lax.broadcasted_iota(jnp.int32, (8, wide), 0) == lax.broadcasted_iota(jnp.int32, (8, wide), 1)
    count = leaves >> level
    index = p * count if count > 0 else p >> level - (leaves.bit_length() - 1)
    hit = jnp.zeros(lanes.shape, jnp.bool_)
    for slot in range(codes.shape[1]):
        row = jnp.broadcast_to(codes[level, slot : slot + 1], (8, wide))
        row = pltpu.roll(row, lax.rem(wide - index, wide), 1)
        code = jnp.sum(jnp.where(diagonal, row, 0).astype(F32), axis=1, keepdims=True)
        hit = hit | (lanes.astype(F32) == code)
    partner = index + cluster + offset
    hit = hit & (partner >= 0) & (partner < wide >> level)
    return jnp.where(hit, 1.0, 0.0)


def lowered(value, table, size):
    rank = value.shape[1]
    out = mm2(value, table, mm_t)
    parts = [out[i : i + size, j : j + rank] for i in range(0, out.shape[0], size) for j in (0, rank)]
    return stack(*parts)


def spread_tables(transfer, couple, spread):
    rank = transfer.shape[-1]
    leaves = spread.shape[1] // rank
    table = lambda level: transfer[level].reshape(2 * rank, rank)
    beside = lambda rows: side(*[rows[i : i + rank] for i in range(0, rows.shape[0], rank)])
    both = stack(transfer[2, 0].astype(F32).T, transfer[2, 1].astype(F32).T, couple[2, 0].astype(F32), couple[2, 3].astype(F32))
    both = beside(lowered(lowered(both, table(1), rank), table(0), rank))
    wide = leaves * rank
    high = both[:, :wide].astype(BF)
    spread[:rank] = high
    spread[rank : 2 * rank] = high
    spread[2 * rank : 3 * rank] = (both[:, :wide] - high.astype(F32)).astype(BF)
    first, second = both[:, wide : wide * 3 // 2].astype(BF), both[:, wide * 3 // 2 :].astype(BF)
    none = jnp.zeros_like(first)
    spread[3 * rank : 4 * rank] = side(first, none)
    spread[4 * rank :] = side(none, second)


def plan_kernel(facing, away, own0, own1, codes, transfer, couple, state, spread, links_out, masks, *lifts):
    rank = transfer.shape[-1]
    levels = masks.shape[0] // 8 - 3
    leaves = spread.shape[1] // rank
    p = lax.axis_index(AXES)
    table = lambda level: transfer[level].reshape(2 * rank, rank)

    mask = [mask_of(codes, level, leaves, p) for level in range(3 + levels)]
    masks[...] = stack(*mask)
    state[...] = couplings(facing, away, own0, own1, mask, transfer, couple)
    spread_tables(transfer, couple, spread)

    for k in range(levels):
        value = couple[3 + k].reshape(4 * rank, rank).astype(F32)
        for i in reversed(range(k)):
            value = mm2(value, transfer[3 + i, (p >> i) & 1], mm_t)
        links_out[4 * rank * k : 4 * rank * (k + 1)] = halves(value, 1)

    value = table(2).astype(F32) * ROOT_HALF
    for k, lift in enumerate(lifts):
        if k > 0:
            b = (p >> (k - 1)) & 1
            value = stack(*[mm2(value, transfer[2 + k, bit]) * ROOT_HALF for bit in (b, 1 - b)])
        lift[...] = halves(value, 1)


def sides_of(facing, away):
    p = lax.axis_index(AXES)
    even = p % 2 == 0
    away = jnp.where((p > 0) & (p < lax.axis_size(AXES) - 1), away, jnp.zeros_like(away))
    return jnp.where(even, away, facing), jnp.where(even, facing, away)


def near_kernel(first, facing, away, x, blocks, near):
    _, _, size, _ = blocks.shape
    leaves = x.shape[1] // size
    rows = x.shape[0]
    left, right = sides_of(facing[: 2 * rows], away[: 2 * rows])
    before = side(left[:rows], left[rows:])
    after = side(right[:rows], right[rows:])
    at = lambda i: before if i < 0 else after if i == leaves else x[:, i * size : (i + 1) * size]
    for i in range(first, first + near.shape[1] // size):
        total = mm_t(at(i), blocks[i, 1])
        total += mm_t(at(i - 1), blocks[i, 0])
        total += mm_t(at(i + 1), blocks[i, 2])
        near[:, (i - first) * size : (i - first + 1) * size] = total


def couplings(facing, away, own0, own1, mask, transfer, couple):
    rank = transfer.shape[-1]
    leaves = mask[0].shape[0]
    rows = own0.shape[0] // leaves * 2
    table = lambda level: transfer[level].reshape(2 * rank, rank)
    left, right = sides_of(facing[...], away[...])
    block = lambda a, i: a[i * rows : (i + 1) * rows]
    lo = slice(0, rank)
    hi = slice(rank, 2 * rank)

    def coupled(level, ext, count):
        weights = mask[level].astype(BF)
        lhs = [side(*[ext[c + 3 + o] for o in OFFSETS]) * weights[c : c + 1] for c in range(count)]
        return mm(stack(*lhs), couple[level].reshape(4 * rank, rank))

    zero = jnp.zeros((rows, rank), BF)
    ext = [zero, block(left, 5)[:, lo], block(left, 5)[:, hi], zero, zero]
    ext += [block(right, 5)[:, lo], block(right, 5)[:, hi], zero]
    far2 = coupled(2, ext, 2)
    ext = [block(left, 4)[:, hi], block(left, 3)[:, lo], block(left, 3)[:, hi]]
    ext += [block(own1, c // 2)[:, (lo, hi)[c % 2]] for c in range(leaves // 2)]
    ext += [block(right, 3)[:, lo], block(right, 3)[:, hi], block(right, 4)[:, hi]]
    far1 = coupled(1, ext, leaves // 2)
    ext = [block(left, 4)[:, lo], block(left, 2)[:, lo], block(left, 2)[:, hi]]
    ext += [block(own0, c // 2)[:, (lo, hi)[c % 2]] for c in range(leaves)]
    ext += [block(right, 2)[:, lo], block(right, 2)[:, hi], block(right, 4)[:, lo]]
    far0 = coupled(0, ext, leaves)
    down = far0 + lowered(far1 + lowered(far2, table(1), rows), table(0), rows)
    return side(*[block(down, c) for c in range(leaves)])


def dense_plan_kernel(
    levels, slots, away, facing, own0, own1, codes, transfer, couple, state, spread, masks, weights, chosen
):
    rank = transfer.shape[-1]
    leaves = spread.shape[1] // rank
    p = lax.axis_index(AXES)

    mask = [mask_of(codes, level, leaves, p) for level in range(3)]
    masks[:8] = mask[2]
    masks[8:] = mask_of(codes, 2, leaves, p ^ 1)
    state[...] = couplings(facing, away, own0, own1, mask, transfer, couple)
    spread_tables(transfer, couple, spread)

    for k in range(levels):
        value = couple[3 + k].reshape(4 * rank, rank).astype(F32)
        for i in reversed(range(1, k)):
            value = mm2(value, transfer[3 + i, (p >> i) & 1], mm_t)
        for j in range(2):
            device = p ^ j
            low = mm2(value, transfer[3, device & 1], mm_t) if k > 0 else value
            hit = mask_of(codes, 3 + k, leaves, device)
            for q in range(4):
                part = low[q * rank : (q + 1) * rank] * hit[:1, q * rank : (q + 1) * rank]
                chosen[2 * k + j, q] = part.astype(BF)
            chosen[2 * k + j, 4] = jnp.zeros((rank, rank), BF)

    lifts = [[transfer[2].reshape(2 * rank, rank).astype(F32) * ROOT_HALF]]
    for k in range(1, levels):
        b = (p >> (k - 1)) & 1
        lifts.append([mm2(a, transfer[2 + k, bit]) * ROOT_HALF for bit in (b, 1 - b) for a in lifts[-1]])
    lifts = [[halves(a, 0) for a in level] for level in lifts]

    for i, slot in enumerate(slots):
        picked = []
        for k in range(levels):
            both = []
            for j in range(2):
                apart = ((p ^ slot) >> k) - ((p ^ j) >> k)
                q = jnp.where(apart < 0, apart + 3, apart)
                q = jnp.where((apart >= -3) & (apart <= 3) & (apart * apart >= 4), q, 4)
                both.append(chosen[2 * k + j, q])
            picked.append(side(*both))
        lift = side(*[lifts[k][slot & ((1 << k) - 1)] for k in range(levels)])
        out = mm(lift, stack(*picked))
        weights[2 * rank * i : 2 * rank * (i + 1)] = halves(out[: 2 * rank] + out[2 * rank :], 1)


def half_kernel(devices, slots, waits, masks, weights, *refs):
    *parts, mine, theirs, gathered = refs
    parts = parts[: len(parts) - waits]
    rank = weights.shape[1] // 4
    rows = mine.shape[0]
    p = lax.axis_index(AXES)
    gathered[...] = jnp.zeros(gathered.shape, BF)
    found = [part[i : i + rows] for part in parts for i in range(0, part.shape[0], rows)]
    for slot, value in zip(slots, found):
        gathered[slot] = value
    top = mm(side(*found), weights[...])
    top = top[:, : 2 * rank] + top[:, 2 * rank :]
    for j, out in ((0, mine), (1, theirs)):
        device = p ^ j
        at = lambda o: gathered[p ^ jnp.clip(device + o, 0, devices - 1)]
        hit = masks[8 * j : 8 * j + 8].astype(BF)
        before = at(-2)[:, rank:] * hit[0:1, :rank]
        after = at(2)[:, :rank] * hit[1:2, 3 * rank :]
        out[...] = side(halves(top[:, j * rank : (j + 1) * rank], 1), before, after)


def leaves_kernel(count, mine, theirs, state, spread, bases, *refs):
    out = refs[-1]
    leaves, rank, size = bases.shape
    near = [(ref, i) for ref in refs[:count] for i in range(0, ref.shape[1], size)]
    a, b = mine[...].astype(F32), theirs[...].astype(F32)
    top = (a[:, :rank] + b[:, :rank]) + (a[:, rank : 2 * rank] + b[:, rank : 2 * rank])
    lhs = side(halves(top, 1), top.astype(BF), (a[:, 2 * rank :] + b[:, 2 * rank :]).astype(BF))
    coef = (mm(lhs, spread[...]) + state[...]).astype(BF)
    for c in range(leaves):
        ref, at = near[c]
        total = mm(coef[:, c * rank : (c + 1) * rank], bases[c]) + ref[:, at : at + size]
        out[:, c * size : (c + 1) * size] = total.astype(BF)


def climb(up, count, transfer, level, bit, rows):
    rank = up.shape[1]
    pairs = up.reshape(count // 2, 2, rows, rank)
    children = [pairs[:, i].reshape(count // 2 * rows, rank) for i in range(2)]
    turned = stack(transfer[level, bit], transfer[level, 1 - bit])
    return mm2(side(*children), turned) * ROOT_HALF


def down_kernel(devices, stages, levels, *refs):
    refs = list(refs)
    slots = slots_of(stages)
    received = refs[: len(slots)]
    refs = refs[len(slots) :]
    lifts = [refs.pop(0) for _ in range(min(levels, 3))]
    state, spread, links, masks, transfer, bases, near, out, gathered, *ups = refs
    leaves, rank, size = bases.shape
    rows = out.shape[0]
    p = lax.axis_index(AXES)

    for part, ref in zip(slots, received):
        for i, slot in enumerate(part):
            gathered[slot] = ref[i * rows : (i + 1) * rows]

    def raised(k, first, count):
        sets = [side(*[gathered[first[i] + j] for j in range(1 << k)]) for i in range(count)]
        up = mm(stack(*sets), lifts[k][...])
        return up[:, :rank] + up[:, rank:]

    if ups:
        count = devices >> 2
        up = raised(2, [4 * i for i in range(count)], count)
        for k in range(3, levels):
            up = climb(up, count, transfer, 2 + k, (p >> (k - 1)) & 1, rows)
            count //= 2
            ups[k - 3][...] = up.reshape(count, rows, rank)
    lhs = []
    for k in range(levels):
        a = p >> k
        n = devices >> k
        places = [a ^ jnp.clip(a + o, 0, n - 1) for o in OFFSETS]
        if k < 3:
            up = raised(k, [place << k for place in places], 4)
            parts = [up[i * rows : (i + 1) * rows] for i in range(4)]
        else:
            parts = [ups[k - 3][place] for place in places]
        lhs.append(side(*parts) * masks[8 * (3 + k) : 8 * (3 + k) + 1])
    top = mm(halves(side(*lhs), 0), links[...])
    top = top[:rows, :rank] + top[:rows, rank:] + top[rows:, :rank] + top[rows:, rank:]

    at = lambda o: gathered[p ^ jnp.clip(p + o, 0, devices - 1)]
    weights = masks[16:24].astype(BF)
    before = at(-2)[:, rank:] * weights[0:1, :rank]
    after = at(2)[:, :rank] * weights[1:2, 3 * rank :]
    lhs = side(halves(top, 1), top.astype(BF), before, after)
    coef = (mm(lhs, spread[...]) + state[...]).astype(BF)
    for c in range(leaves):
        cols = slice(c * size, (c + 1) * size)
        out[:, cols] = (mm(coef[:, c * rank : (c + 1) * rank], bases[c]) + near[:, cols]).astype(BF)


def inside(x):
    return pltpu.with_memory_space_constraint(x, pltpu.VMEM)


def outside(x):
    return pltpu.with_memory_space_constraint(x, pltpu.HBM)


def shards(rhs, bases, near_blocks, transfer, couple, codes):
    rows = rhs.shape[0]
    leaves, rank, size = bases.shape
    devices = lax.axis_size(AXES)
    stages = stages_of(devices)
    levels = devices.bit_length() - 2
    params = pltpu.CompilerParams(vmem_limit_bytes=16 << 20)

    def call(kernel, shapes, operands, name, flops=0, place=inside, **more):
        single = not isinstance(shapes, list)
        return pl.pallas_call(
            kernel,
            out_shape=shapes if single else list(shapes),
            compiler_params=params,
            cost_estimate=pl.CostEstimate(flops=flops, bytes_accessed=1 << 20, transcendentals=0),
            name=name,
            **more,
        )(*map(place, operands))

    x, bases, facing, away, own0, own1, own2 = call(
        first_kernel,
        [
            pltpu.VMEM(rhs.shape, BF),
            pltpu.VMEM(bases.shape, BF),
            pltpu.VMEM((6 * rows, 2 * rank), BF),
            pltpu.VMEM((6 * rows, 2 * rank), BF),
            pltpu.VMEM((leaves // 2 * rows, 2 * rank), BF),
            pltpu.VMEM((leaves // 4 * rows, 2 * rank), BF),
            pltpu.VMEM((rows, 2 * rank), BF),
        ],
        (rhs, bases, transfer),
        "first",
        1 << 32,
        place=outside,
        in_specs=[pl.BlockSpec(memory_space=pl.ANY)] * 3,
        scratch_shapes=[pltpu.VMEM((2, 2, rank, rank), BF), pltpu.SemaphoreType.DMA((3,))],
    )

    facing = exchanged(facing, 1)
    away = across_pairs(away)

    dense = levels <= 3
    if dense:
        slots = [slot for part in slots_of(stages)[:-1] for slot in part]
        state, spread, masks, weights = call(
            functools.partial(dense_plan_kernel, levels, slots),
            [
                pltpu.VMEM((rows, leaves * rank), F32),
                pltpu.VMEM((5 * rank, leaves * rank), BF),
                pltpu.VMEM((16, 4 * rank), F32),
                pltpu.VMEM((2 * rank * len(slots), 4 * rank), BF),
            ],
            (away, facing, own0, own1, codes, transfer, couple),
            "plan",
            1 << 30,
            scratch_shapes=[pltpu.VMEM((2 * levels, 5, rank, rank), BF)],
        )
    else:
        lifts = [pltpu.VMEM(((2 << k) * rank, 2 * rank), BF) for k in range(min(levels, 3))]
        state, spread, links, masks, *lifts = call(
            plan_kernel,
            [
                pltpu.VMEM((rows, leaves * rank), F32),
                pltpu.VMEM((5 * rank, leaves * rank), BF),
                pltpu.VMEM((levels * 4 * rank, 2 * rank), BF),
                pltpu.VMEM((8 * (3 + levels), 4 * rank), F32),
                *lifts,
            ],
            (facing, away, own0, own1, codes, transfer, couple),
            "plan",
            1 << 30,
        )

    def near_of(first, count):
        return call(
            functools.partial(near_kernel, first),
            pltpu.VMEM((rows, count * size), F32),
            (facing, away, x, near_blocks),
            "near_field",
            3 * count * rows * size * size * 2,
        )

    some = leaves * SHARE // 8 if dense else 0
    near = (near_of(0, some),) if some else ()
    gathered = own2
    received = [own2]
    for group in stages[:-1]:
        got = [exchanged(gathered, m) for m in group]
        received += got
        if group is not stages[-2]:
            gathered = stack(gathered, *got)
    if dense:
        mine, theirs = call(
            functools.partial(half_kernel, devices, slots, len(near)),
            [pltpu.VMEM((rows, 4 * rank), BF), pltpu.VMEM((rows, 4 * rank), BF)],
            (masks, weights, *received, *near),
            "half",
            scratch_shapes=[pltpu.VMEM((devices, rows, 2 * rank), BF)],
        )
        theirs = exchanged(theirs, 1)
    else:
        parts = (gathered, *got) if len(stages) > 1 else (gathered,)
        pay = call(
            pack_kernel,
            pltpu.VMEM((sum(part.shape[0] for part in parts), 2 * rank), BF),
            (masks, *parts),
            "pack",
        )
        received.append(exchanged(pay, 1))

    near = (*near, near_of(some, leaves - some))
    if dense:
        return call(
            functools.partial(leaves_kernel, len(near)),
            jax.ShapeDtypeStruct((rows, leaves * size), BF),
            (mine, theirs, state, spread, bases, *near, *received, masks, weights, transfer),
            "leaves",
        )
    return call(
        functools.partial(down_kernel, devices, stages, levels),
        jax.ShapeDtypeStruct((rows, leaves * size), BF),
        (*received, *lifts, state, spread, links, masks, transfer, bases, *near),
        "down_sweep",
        scratch_shapes=[pltpu.VMEM((devices, rows, 2 * rank), BF)]
        + [pltpu.VMEM((devices >> k, rows, rank), F32) for k in range(3, levels)],
    )


def solution(mesh):
    return jax.shard_map(
        shards,
        mesh=mesh,
        in_specs=(
            P(None, ("groups", "leaf", "sub")),
            P(("groups", "leaf", "sub"), None, None),
            P(("groups", "leaf", "sub"), None, None, None),
            P(),
            P(),
            P(),
        ),
        out_specs=P(None, ("groups", "leaf", "sub")),
        check_vma=False,
    )
```

```python
import functools

import jax
import jax.numpy as jnp
from jax import lax
from jax.experimental import pallas as pl
from jax.experimental.pallas import tpu as pltpu
from jax.sharding import PartitionSpec as P

ROOT_HALF = 0.7071067811865476
OFFSETS = (-3, -2, 2, 3)
AXES = ("leaf", "sub")
BF = jnp.bfloat16
F32 = jnp.float32
LANES = 64
SHARE = 4


def mm(a, b):
    return lax.dot_general(a, b, (((1,), (0,)), ((), ())), preferred_element_type=F32)


def mm_t(a, b):
    return lax.dot_general(a, b, (((1,), (1,)), ((), ())), preferred_element_type=F32)


def split(a):
    high = a.astype(BF)
    low = (a - high.astype(F32)).astype(BF)
    return jnp.concatenate([high, low], axis=0)


def mm2(a, b, product=mm):
    out = product(split(a), b)
    return out[: a.shape[0]] + out[a.shape[0] :]


def halves(a, axis):
    high = a.astype(BF)
    return jnp.concatenate([high, (a - high.astype(F32)).astype(BF)], axis=axis)


def side(*parts):
    return jnp.concatenate(parts, axis=1)


def stack(*parts):
    return jnp.concatenate(parts, axis=0)


def stages_of(devices):
    bits = [1 << b for b in range(1, devices.bit_length() - 1)]
    rounds = [(bits.pop() | 1,)] if len(bits) % 2 else []
    while bits:
        high, low = bits.pop(), bits.pop()
        rounds.append((low | 1, high | 1, low | high))
    return rounds + [(1,)]


def slots_of(stages):
    held = [[0]]
    for masks in stages:
        so_far = [slot for part in held for slot in part]
        held += [[slot ^ m for slot in so_far] for m in masks]
    return held


def exchanged(x, apart):
    devices = lax.axis_size(AXES)
    return lax.ppermute(x, AXES, [(i, i ^ apart) for i in range(devices)])


def across_pairs(x):
    groups, devices = lax.axis_size("groups"), lax.axis_size(AXES)
    pairs = []
    for g in range(groups):
        for i in range(devices):
            j = i + 1 if i % 2 else i - 1
            to = (g, j) if 0 <= j < devices else ((g + 1) % groups, i)
            pairs.append((g * devices + i, to[0] * devices + to[1]))
    return lax.ppermute(x, ("groups", *AXES), pairs)


def first_kernel(rhs_hbm, bases_hbm, transfer_hbm, x, bases, facing, away, own0, own1, own2, low, sems):
    leaves, rank, size = bases.shape
    rows = x.shape[0]
    pairs = (
        (transfer_hbm.at[pl.ds(0, 2)], low),
        (bases_hbm, bases),
        (rhs_hbm, x),
    )
    copies = [pltpu.make_async_copy(*pair, sems.at[i]) for i, pair in enumerate(pairs)]
    for copy in copies:
        copy.start()
    copies[0].wait()
    table = low[0].reshape(2 * rank, rank)
    product = halves(stack(mm(table, low[1, 0]), mm(table, low[1, 1])) * (ROOT_HALF * ROOT_HALF), 1)
    copies[1].wait()
    copies[2].wait()
    at = lambda i: x[:, i * size : (i + 1) * size]
    first = lax.broadcasted_iota(jnp.int32, (rows, 2 * rank), 1) < rank
    parts = []
    for i in range(0, leaves, 2):
        both = mm_t(stack(at(i), at(i + 1)), bases[i : i + 2].reshape(2 * rank, size))
        parts.append(jnp.where(first, both[:rows], both[rows:]))
    leaf_coef = stack(*parts)
    fours = stack(*[side(parts[i], parts[i + 1]) for i in range(0, leaves // 2, 2)])
    up = mm(halves(fours, 0), product)
    count = fours.shape[0]
    up = up[:count, :rank] + up[:count, rank:] + up[count:, :rank]
    own2[...] = side(*[up[i : i + rows] for i in range(0, count, rows)]).astype(BF)
    u2 = own2

    own0[...] = leaf_coef.astype(BF)
    up1 = mm2(leaf_coef, table) * ROOT_HALF
    up1 = [up1[i : i + rows] for i in range(0, up1.shape[0], rows)]
    own1[...] = stack(*[side(up1[i], up1[i + 1]) for i in range(0, len(up1), 2)]).astype(BF)
    end = x.shape[1]
    half = size // 2
    last0, last1 = own0.shape[0] - rows, own1.shape[0] - rows
    right = stack(
        x[:, end - size : end - half],
        x[:, end - half :],
        own0[last0:],
        own1[last1:],
        side(own0[last0 - rows : last0, rank:], own1[last1 - rows : last1, rank:]),
        u2[...],
    )
    left = stack(
        x[:, :half],
        x[:, half:size],
        own0[:rows],
        own1[:rows],
        side(own0[rows : 2 * rows, :rank], own1[rows : 2 * rows, :rank]),
        u2[...],
    )
    even = lax.axis_index(AXES) % 2 == 0
    facing[...] = jnp.where(even, right, left)
    away[...] = jnp.where(even, left, right)


def pack_kernel(after, *refs):
    *parts, out = refs
    at = 0
    for part in parts:
        out[at : at + part.shape[0]] = part[...]
        at += part.shape[0]


def mask_of(codes, level, leaves, p):
    wide = codes.shape[2]
    lanes = lax.broadcasted_iota(jnp.int32, (8, 4 * LANES), 1) // LANES
    offset = jnp.where(lanes < 2, lanes - 3, lanes)
    cluster = lax.broadcasted_iota(jnp.int32, (8, 4 * LANES), 0)
    diagonal = lax.broadcasted_iota(jnp.int32, (8, wide), 0) == lax.broadcasted_iota(jnp.int32, (8, wide), 1)
    count = leaves >> level
    index = p * count if count > 0 else p >> level - (leaves.bit_length() - 1)
    hit = jnp.zeros(lanes.shape, jnp.bool_)
    for slot in range(codes.shape[1]):
        row = jnp.broadcast_to(codes[level, slot : slot + 1], (8, wide))
        row = pltpu.roll(row, lax.rem(wide - index, wide), 1)
        code = jnp.sum(jnp.where(diagonal, row, 0).astype(F32), axis=1, keepdims=True)
        hit = hit | (lanes.astype(F32) == code)
    partner = index + cluster + offset
    hit = hit & (partner >= 0) & (partner < wide >> level)
    return jnp.where(hit, 1.0, 0.0)


def lowered(value, table, size):
    rank = value.shape[1]
    out = mm2(value, table, mm_t)
    parts = [out[i : i + size, j : j + rank] for i in range(0, out.shape[0], size) for j in (0, rank)]
    return stack(*parts)


def spread_tables(transfer, couple, spread):
    rank = transfer.shape[-1]
    leaves = spread.shape[1] // rank
    table = lambda level: transfer[level].reshape(2 * rank, rank)
    beside = lambda rows: side(*[rows[i : i + rank] for i in range(0, rows.shape[0], rank)])
    both = stack(transfer[2, 0].astype(F32).T, transfer[2, 1].astype(F32).T, couple[2, 0].astype(F32), couple[2, 3].astype(F32))
    both = beside(lowered(lowered(both, table(1), rank), table(0), rank))
    wide = leaves * rank
    high = both[:, :wide].astype(BF)
    spread[:rank] = high
    spread[rank : 2 * rank] = high
    spread[2 * rank : 3 * rank] = (both[:, :wide] - high.astype(F32)).astype(BF)
    first, second = both[:, wide : wide * 3 // 2].astype(BF), both[:, wide * 3 // 2 :].astype(BF)
    none = jnp.zeros_like(first)
    spread[3 * rank : 4 * rank] = side(first, none)
    spread[4 * rank :] = side(none, second)


def plan_kernel(facing, away, own0, own1, codes, transfer, couple, state, spread, links_out, masks, *lifts):
    rank = transfer.shape[-1]
    levels = masks.shape[0] // 8 - 3
    leaves = spread.shape[1] // rank
    p = lax.axis_index(AXES)
    table = lambda level: transfer[level].reshape(2 * rank, rank)

    mask = [mask_of(codes, level, leaves, p) for level in range(3 + levels)]
    masks[...] = stack(*mask)
    state[...] = couplings(facing, away, own0, own1, mask, transfer, couple)
    spread_tables(transfer, couple, spread)

    for k in range(levels):
        value = couple[3 + k].reshape(4 * rank, rank).astype(F32)
        for i in reversed(range(k)):
            value = mm2(value, transfer[3 + i, (p >> i) & 1], mm_t)
        links_out[4 * rank * k : 4 * rank * (k + 1)] = halves(value, 1)

    value = table(2).astype(F32) * ROOT_HALF
    for k, lift in enumerate(lifts):
        if k > 0:
            b = (p >> (k - 1)) & 1
            value = stack(*[mm2(value, transfer[2 + k, bit]) * ROOT_HALF for bit in (b, 1 - b)])
        lift[...] = halves(value, 1)


def sides_of(facing, away):
    p = lax.axis_index(AXES)
    even = p % 2 == 0
    away = jnp.where((p > 0) & (p < lax.axis_size(AXES) - 1), away, jnp.zeros_like(away))
    return jnp.where(even, away, facing), jnp.where(even, facing, away)


def near_kernel(first, facing, away, x, blocks, near):
    _, _, size, _ = blocks.shape
    leaves = x.shape[1] // size
    rows = x.shape[0]
    left, right = sides_of(facing[: 2 * rows], away[: 2 * rows])
    before = side(left[:rows], left[rows:])
    after = side(right[:rows], right[rows:])
    at = lambda i: before if i < 0 else after if i == leaves else x[:, i * size : (i + 1) * size]
    for i in range(first, first + near.shape[1] // size):
        total = mm_t(at(i), blocks[i, 1])
        total += mm_t(at(i - 1), blocks[i, 0])
        total += mm_t(at(i + 1), blocks[i, 2])
        near[:, (i - first) * size : (i - first + 1) * size] = total


def couplings(facing, away, own0, own1, mask, transfer, couple):
    rank = transfer.shape[-1]
    leaves = mask[0].shape[0]
    rows = own0.shape[0] // leaves * 2
    table = lambda level: transfer[level].reshape(2 * rank, rank)
    left, right = sides_of(facing[...], away[...])
    block = lambda a, i: a[i * rows : (i + 1) * rows]
    lo = slice(0, rank)
    hi = slice(rank, 2 * rank)

    def coupled(level, ext, count):
        weights = mask[level].astype(BF)
        lhs = [side(*[ext[c + 3 + o] for o in OFFSETS]) * weights[c : c + 1] for c in range(count)]
        return mm(stack(*lhs), couple[level].reshape(4 * rank, rank))

    zero = jnp.zeros((rows, rank), BF)
    ext = [zero, block(left, 5)[:, lo], block(left, 5)[:, hi], zero, zero]
    ext += [block(right, 5)[:, lo], block(right, 5)[:, hi], zero]
    far2 = coupled(2, ext, 2)
    ext = [block(left, 4)[:, hi], block(left, 3)[:, lo], block(left, 3)[:, hi]]
    ext += [block(own1, c // 2)[:, (lo, hi)[c % 2]] for c in range(leaves // 2)]
    ext += [block(right, 3)[:, lo], block(right, 3)[:, hi], block(right, 4)[:, hi]]
    far1 = coupled(1, ext, leaves // 2)
    ext = [block(left, 4)[:, lo], block(left, 2)[:, lo], block(left, 2)[:, hi]]
    ext += [block(own0, c // 2)[:, (lo, hi)[c % 2]] for c in range(leaves)]
    ext += [block(right, 2)[:, lo], block(right, 2)[:, hi], block(right, 4)[:, lo]]
    far0 = coupled(0, ext, leaves)
    down = far0 + lowered(far1 + lowered(far2, table(1), rows), table(0), rows)
    return side(*[block(down, c) for c in range(leaves)])


def dense_plan_kernel(
    levels, slots, away, facing, own0, own1, codes, transfer, couple, state, spread, masks, weights, chosen
):
    rank = transfer.shape[-1]
    leaves = spread.shape[1] // rank
    p = lax.axis_index(AXES)

    mask = [mask_of(codes, level, leaves, p) for level in range(3)]
    masks[:8] = mask[2]
    masks[8:] = mask_of(codes, 2, leaves, p ^ 1)
    state[...] = couplings(facing, away, own0, own1, mask, transfer, couple)
    spread_tables(transfer, couple, spread)

    for k in range(levels):
        value = couple[3 + k].reshape(4 * rank, rank).astype(F32)
        for i in reversed(range(1, k)):
            value = mm2(value, transfer[3 + i, (p >> i) & 1], mm_t)
        for j in range(2):
            device = p ^ j
            low = mm2(value, transfer[3, device & 1], mm_t) if k > 0 else value
            hit = mask_of(codes, 3 + k, leaves, device)
            for q in range(4):
                part = low[q * rank : (q + 1) * rank] * hit[:1, q * rank : (q + 1) * rank]
                chosen[2 * k + j, q] = part.astype(BF)
            chosen[2 * k + j, 4] = jnp.zeros((rank, rank), BF)

    lifts = [[transfer[2].reshape(2 * rank, rank).astype(F32) * ROOT_HALF]]
    for k in range(1, levels):
        b = (p >> (k - 1)) & 1
        lifts.append([mm2(a, transfer[2 + k, bit]) * ROOT_HALF for bit in (b, 1 - b) for a in lifts[-1]])
    lifts = [[halves(a, 0) for a in level] for level in lifts]

    for i, slot in enumerate(slots):
        picked = []
        for k in range(levels):
            both = []
            for j in range(2):
                apart = ((p ^ slot) >> k) - ((p ^ j) >> k)
                q = jnp.where(apart < 0, apart + 3, apart)
                q = jnp.where((apart >= -3) & (apart <= 3) & (apart * apart >= 4), q, 4)
                both.append(chosen[2 * k + j, q])
            picked.append(side(*both))
        lift = side(*[lifts[k][slot & ((1 << k) - 1)] for k in range(levels)])
        out = mm(lift, stack(*picked))
        weights[2 * rank * i : 2 * rank * (i + 1)] = halves(out[: 2 * rank] + out[2 * rank :], 1)


def half_kernel(devices, slots, waits, masks, weights, *refs):
    *parts, mine, theirs, gathered = refs
    parts = parts[: len(parts) - waits]
    rank = weights.shape[1] // 4
    rows = mine.shape[0]
    p = lax.axis_index(AXES)
    gathered[...] = jnp.zeros(gathered.shape, BF)
    found = [part[i : i + rows] for part in parts for i in range(0, part.shape[0], rows)]
    for slot, value in zip(slots, found):
        gathered[slot] = value
    top = mm(side(*found), weights[...])
    top = top[:, : 2 * rank] + top[:, 2 * rank :]
    for j, out in ((0, mine), (1, theirs)):
        device = p ^ j
        at = lambda o: gathered[p ^ jnp.clip(device + o, 0, devices - 1)]
        hit = masks[8 * j : 8 * j + 8].astype(BF)
        before = at(-2)[:, rank:] * hit[0:1, :rank]
        after = at(2)[:, :rank] * hit[1:2, 3 * rank :]
        out[...] = side(halves(top[:, j * rank : (j + 1) * rank], 1), before, after)


def leaves_kernel(count, mine, theirs, state, spread, bases, *refs):
    out = refs[-1]
    leaves, rank, size = bases.shape
    near = [(ref, i) for ref in refs[:count] for i in range(0, ref.shape[1], size)]
    a, b = mine[...].astype(F32), theirs[...].astype(F32)
    top = (a[:, :rank] + b[:, :rank]) + (a[:, rank : 2 * rank] + b[:, rank : 2 * rank])
    lhs = side(halves(top, 1), top.astype(BF), (a[:, 2 * rank :] + b[:, 2 * rank :]).astype(BF))
    coef = (mm(lhs, spread[...]) + state[...]).astype(BF)
    for c in range(leaves):
        ref, at = near[c]
        total = mm(coef[:, c * rank : (c + 1) * rank], bases[c]) + ref[:, at : at + size]
        out[:, c * size : (c + 1) * size] = total.astype(BF)


def climb(up, count, transfer, level, bit, rows):
    rank = up.shape[1]
    pairs = up.reshape(count // 2, 2, rows, rank)
    children = [pairs[:, i].reshape(count // 2 * rows, rank) for i in range(2)]
    turned = stack(transfer[level, bit], transfer[level, 1 - bit])
    return mm2(side(*children), turned) * ROOT_HALF


def down_kernel(devices, stages, levels, *refs):
    refs = list(refs)
    slots = slots_of(stages)
    received = refs[: len(slots)]
    refs = refs[len(slots) :]
    lifts = [refs.pop(0) for _ in range(min(levels, 3))]
    state, spread, links, masks, transfer, bases, near, out, gathered, *ups = refs
    leaves, rank, size = bases.shape
    rows = out.shape[0]
    p = lax.axis_index(AXES)

    for part, ref in zip(slots, received):
        for i, slot in enumerate(part):
            gathered[slot] = ref[i * rows : (i + 1) * rows]

    def raised(k, first, count):
        sets = [side(*[gathered[first[i] + j] for j in range(1 << k)]) for i in range(count)]
        up = mm(stack(*sets), lifts[k][...])
        return up[:, :rank] + up[:, rank:]

    if ups:
        count = devices >> 2
        up = raised(2, [4 * i for i in range(count)], count)
        for k in range(3, levels):
            up = climb(up, count, transfer, 2 + k, (p >> (k - 1)) & 1, rows)
            count //= 2
            ups[k - 3][...] = up.reshape(count, rows, rank)
    lhs = []
    for k in range(levels):
        a = p >> k
        n = devices >> k
        places = [a ^ jnp.clip(a + o, 0, n - 1) for o in OFFSETS]
        if k < 3:
            up = raised(k, [place << k for place in places], 4)
            parts = [up[i * rows : (i + 1) * rows] for i in range(4)]
        else:
            parts = [ups[k - 3][place] for place in places]
        lhs.append(side(*parts) * masks[8 * (3 + k) : 8 * (3 + k) + 1])
    top = mm(halves(side(*lhs), 0), links[...])
    top = top[:rows, :rank] + top[:rows, rank:] + top[rows:, :rank] + top[rows:, rank:]

    at = lambda o: gathered[p ^ jnp.clip(p + o, 0, devices - 1)]
    weights = masks[16:24].astype(BF)
    before = at(-2)[:, rank:] * weights[0:1, :rank]
    after = at(2)[:, :rank] * weights[1:2, 3 * rank :]
    lhs = side(halves(top, 1), top.astype(BF), before, after)
    coef = (mm(lhs, spread[...]) + state[...]).astype(BF)
    for c in range(leaves):
        cols = slice(c * size, (c + 1) * size)
        out[:, cols] = (mm(coef[:, c * rank : (c + 1) * rank], bases[c]) + near[:, cols]).astype(BF)


def inside(x):
    return pltpu.with_memory_space_constraint(x, pltpu.VMEM)


def outside(x):
    return pltpu.with_memory_space_constraint(x, pltpu.HBM)


def shards(rhs, bases, near_blocks, transfer, couple, codes):
    rows = rhs.shape[0]
    leaves, rank, size = bases.shape
    devices = lax.axis_size(AXES)
    stages = stages_of(devices)
    levels = devices.bit_length() - 2
    params = pltpu.CompilerParams(vmem_limit_bytes=16 << 20)

    def call(kernel, shapes, operands, name, flops=0, place=inside, **more):
        single = not isinstance(shapes, list)
        return pl.pallas_call(
            kernel,
            out_shape=shapes if single else list(shapes),
            compiler_params=params,
            cost_estimate=pl.CostEstimate(flops=flops, bytes_accessed=1 << 20, transcendentals=0),
            name=name,
            **more,
        )(*map(place, operands))

    x, bases, facing, away, own0, own1, own2 = call(
        first_kernel,
        [
            pltpu.VMEM(rhs.shape, BF),
            pltpu.VMEM(bases.shape, BF),
            pltpu.VMEM((6 * rows, 2 * rank), BF),
            pltpu.VMEM((6 * rows, 2 * rank), BF),
            pltpu.VMEM((leaves // 2 * rows, 2 * rank), BF),
            pltpu.VMEM((leaves // 4 * rows, 2 * rank), BF),
            pltpu.VMEM((rows, 2 * rank), BF),
        ],
        (rhs, bases, transfer),
        "first",
        1 << 32,
        place=outside,
        in_specs=[pl.BlockSpec(memory_space=pl.ANY)] * 3,
        scratch_shapes=[pltpu.VMEM((2, 2, rank, rank), BF), pltpu.SemaphoreType.DMA((3,))],
    )

    facing = exchanged(facing, 1)
    away = across_pairs(away)

    dense = levels <= 3
    if dense:
        slots = [slot for part in slots_of(stages)[:-1] for slot in part]
        state, spread, masks, weights = call(
            functools.partial(dense_plan_kernel, levels, slots),
            [
                pltpu.VMEM((rows, leaves * rank), F32),
                pltpu.VMEM((5 * rank, leaves * rank), BF),
                pltpu.VMEM((16, 4 * rank), F32),
                pltpu.VMEM((2 * rank * len(slots), 4 * rank), BF),
            ],
            (away, facing, own0, own1, codes, transfer, couple),
            "plan",
            1 << 30,
            scratch_shapes=[pltpu.VMEM((2 * levels, 5, rank, rank), BF)],
        )
    else:
        lifts = [pltpu.VMEM(((2 << k) * rank, 2 * rank), BF) for k in range(min(levels, 3))]
        state, spread, links, masks, *lifts = call(
            plan_kernel,
            [
                pltpu.VMEM((rows, leaves * rank), F32),
                pltpu.VMEM((5 * rank, leaves * rank), BF),
                pltpu.VMEM((levels * 4 * rank, 2 * rank), BF),
                pltpu.VMEM((8 * (3 + levels), 4 * rank), F32),
                *lifts,
            ],
            (facing, away, own0, own1, codes, transfer, couple),
            "plan",
            1 << 30,
        )

    def near_of(first, count):
        return call(
            functools.partial(near_kernel, first),
            pltpu.VMEM((rows, count * size), F32),
            (facing, away, x, near_blocks),
            "near_field",
            3 * count * rows * size * size * 2,
        )

    some = leaves * SHARE // 8 if dense else 0
    near = (near_of(0, some),) if some else ()
    gathered = own2
    received = [own2]
    for group in stages[:-1]:
        got = [exchanged(gathered, m) for m in group]
        received += got
        if group is not stages[-2]:
            gathered = stack(gathered, *got)
    if dense:
        mine, theirs = call(
            functools.partial(half_kernel, devices, slots, len(near)),
            [pltpu.VMEM((rows, 4 * rank), BF), pltpu.VMEM((rows, 4 * rank), BF)],
            (masks, weights, *received, *near),
            "half",
            scratch_shapes=[pltpu.VMEM((devices, rows, 2 * rank), BF)],
        )
        theirs = exchanged(theirs, 1)
    else:
        parts = (gathered, *got) if len(stages) > 1 else (gathered,)
        pay = call(
            pack_kernel,
            pltpu.VMEM((sum(part.shape[0] for part in parts), 2 * rank), BF),
            (masks, *parts),
            "pack",
        )
        received.append(exchanged(pay, 1))

    near = (*near, near_of(some, leaves - some))
    if dense:
        return call(
            functools.partial(leaves_kernel, len(near)),
            jax.ShapeDtypeStruct((rows, leaves * size), BF),
            (mine, theirs, state, spread, bases, *near, *received, masks, weights, transfer),
            "leaves",
        )
    return call(
        functools.partial(down_kernel, devices, stages, levels),
        jax.ShapeDtypeStruct((rows, leaves * size), BF),
        (*received, *lifts, state, spread, links, masks, transfer, bases, *near),
        "down_sweep",
        scratch_shapes=[pltpu.VMEM((devices, rows, 2 * rank), BF)]
        + [pltpu.VMEM((devices >> k, rows, rank), F32) for k in range(3, levels)],
    )


def solution(mesh):
    return jax.shard_map(
        shards,
        mesh=mesh,
        in_specs=(
            P(None, ("groups", "leaf", "sub")),
            P(("groups", "leaf", "sub"), None, None),
            P(("groups", "leaf", "sub"), None, None, None),
            P(),
            P(),
            P(),
        ),
        out_specs=P(None, ("groups", "leaf", "sub")),
        check_vma=False,
    )
```
